256 devices in a mesh: pipe: 8 (over z_hi, core), tensor: 32 (over x, z_lo, y).
Axes of the slice: x: 4, y: 4, z: 8 (z_hi: 4, z_lo: 2; z = z_hi * 2 + z_lo), core: 2. Of those that a mesh axis runs over, the one named last changes fastest.
Arguments:
- incoming: bfloat16 [6144, 8192], P('tensor', 'pipe'), may hold values from -12 to 12
- scene_lengths: int32 [8, 4], P('pipe'), may hold values from 1 to 512, 1024 in all within a row
- attn_gain: float32 [8, 6144], P('pipe'), may hold values from 0.1 to 1.9
- query_weight: bfloat16 [8, 6144, 6144], P('pipe', 'tensor'), may hold values from -0.5 to 0.5
- key_weight: bfloat16 [8, 6144, 6144], P('pipe', 'tensor'), may hold values from -0.5 to 0.5
- value_weight: bfloat16 [8, 6144, 6144], P('pipe', 'tensor'), may hold values from -2 to 2
- output_weight: bfloat16 [8, 6144, 6144], P('pipe', 'tensor'), may hold values from -2 to 2
- ffn_gain: float32 [8, 6144], P('pipe', 'tensor'), may hold values from 0.1 to 1.9
- up_first: bfloat16 [8, 32, 192, 768], P('pipe', 'tensor'), may hold values from -0.4375 to 0.4375
- up_second: bfloat16 [8, 32, 768, 768], P('pipe', 'tensor'), may hold values from -0.4375 to 0.4375
- down_first: bfloat16 [8, 32, 768, 768], P('pipe', 'tensor'), may hold values from -0.21875 to 0.21875
- down_second: bfloat16 [8, 32, 768, 192], P('pipe', 'tensor'), may hold values from -0.875 to 0.875
Outputs:
- outgoing: bfloat16 [6144, 8192], P('tensor', 'pipe')
The draws below stay inside these ranges and needn't reach their ends.
Inputs may be any that keep to these rules, and one draw needn't show every extreme that they name: `scene_lengths`: row s holds the lengths of the 4 scenes packed in order into the 1024 tokens that section s processes; they sum to 1024.
All inputs are finite; a program needn't handle non-finite values.
Results may differ from the reference program's by a relative error of at most 0.027.
Values may be sent and summed in bfloat16 or wider, within the bound.
No kernel may reach another device: no remote copies, remote signals or barrier semaphores. Data moves between devices by JAX's collectives and lax.ppermute only.
A program may use at most 128 MiB of HBM per device.

```python
import math
import jax
import jax.numpy as jnp
import numpy as np
from jax import lax

D = 6144
HEADS = 32
HEAD = 192
BLOCKS = 32
SCENES = 4
TOK = 1024
SEGMENTS = 8
BLOCK_IN = 192
BLOCK_OUT = 768
PIECE = 24
GROUP_HEADS = 1
N_TENSOR = 32


def shared_base(key):
    return jax.random.normal(jax.random.fold_in(key, 101), (SEGMENTS, D, D), jnp.float32)


def head_pattern(key):
    key_common, key_noise = jax.random.split(key, 2)
    common = jnp.clip(jax.random.normal(key_common, (SEGMENTS, 1, HEAD, D), jnp.float32), -6.0, 6.0)
    common = jnp.broadcast_to(common, (SEGMENTS, HEADS, HEAD, D)).reshape(SEGMENTS, D, D)
    noise = jnp.clip(jax.random.normal(key_noise, (SEGMENTS, D, D), jnp.float32), -6.0, 6.0)
    return 0.837 * common + 0.548 * noise


def draw_incoming(key, part):
    key = jax.random.fold_in(key, 3)
    key_main, key_column = jax.random.split(key, 2)
    feature = jnp.arange(D, dtype=jnp.float32)[:, None]
    jitter = jax.random.uniform(key_column, (D, 1), jnp.float32, minval=-0.35, maxval=0.35)
    feature_scale = jnp.exp(math.log(10.0) * feature / (D - 1) + jitter)
    values = jax.random.normal(key_main, (D, SEGMENTS * TOK), jnp.float32) * feature_scale * 0.5
    return jnp.clip(values, -12.0, 12.0).astype(jnp.bfloat16)


def draw_query_weight(key, part):
    values = shared_base(key) * D ** (-0.5)
    return jnp.clip(values, -0.5, 0.5).astype(jnp.bfloat16)


def draw_key_weight(key, part):
    key = jax.random.fold_in(key, 6)
    values = jax.random.normal(key, (SEGMENTS, D, D), jnp.float32) * D ** (-0.5)
    return jnp.clip(values, -0.5, 0.5).astype(jnp.bfloat16)


def draw_value_weight(key, part):
    key = jax.random.fold_in(key, 7)
    values = head_pattern(key) * D ** (-0.5)
    return jnp.clip(values, -2.0, 2.0).astype(jnp.bfloat16)


def draw_output_weight(key, part):
    key = jax.random.fold_in(key, 8)
    values = head_pattern(key) * 3.2 * D ** (-0.5)
    return jnp.clip(values, -2.0, 2.0).astype(jnp.bfloat16)


def shard_levels(own_key, shape, pieces, smallest, high):
    loudness, own = 1.0, jax.random.fold_in(own_key, 6)
    for position, shards_of in pieces:
        draws = jnp.exp(jax.random.uniform(jax.random.fold_in(own, position), (shards_of,), jnp.float32, smallest / len(pieces), high / len(pieces)))
        loudness = loudness * jnp.repeat(draws, shape[position] // shards_of).reshape([-1 if axis == position else 1 for axis in range(len(shape))])
    return loudness


def split_up(count, total, bound, slope):
    weights = [(1 << 20) // math.isqrt(rank ** slope) + 1 for rank in range(2, count + 1)]
    surplus, counts = total - bound - (count - 1), [1] * (count - 1)
    while surplus > 0:
        movable = [i for i in range(count - 1) if counts[i] < bound]
        pool, left = sum([weights[i] for i in movable]), surplus
        for i in movable:
            more = min(bound - counts[i], max(1, left * weights[i] // pool), surplus)
            counts[i] = counts[i] + more
            surplus = surplus - more
    return np.array([bound] + counts)


def ragged(stream_key, number_of, total, limit, slope):
    if number_of == 2:
        one = jax.random.randint(stream_key, (), max(1, total - limit), min(limit, total - 1) + 1)
        return jnp.stack([one, total - one])
    lengths = jnp.asarray(split_up(number_of, total, limit, slope), jnp.int32)
    couples = (number_of - 1) // 2
    donor, receiver = lengths[1:1 + 2 * couples:2], lengths[2:2 + 2 * couples:2]
    slack = jnp.minimum(donor - 1, limit - receiver)
    passed = jax.random.randint(jax.random.fold_in(stream_key, 1), (couples,), 0, 1 << 20) % (slack + 1)
    lengths = lengths.at[1:1 + 2 * couples:2].set(donor - passed).at[2:2 + 2 * couples:2].set(receiver + passed)
    return lengths[jax.random.permutation(jax.random.fold_in(stream_key, 2), number_of)]


def normal_values(key, dims, scale, bound, pieces=(), kind=jnp.bfloat16):
    drawn = jax.random.normal(key, dims, jnp.float32) * scale
    if len(pieces) > 0:
        drawn = shard_levels(key, dims, pieces, -0.22, 0.18) * drawn
    return jnp.clip(drawn, min=-bound, max=bound).astype(kind)


def setup_inputs(seed: int = 0) -> dict:
    key_of = jax.random.split(jax.random.key(seed), 13)
    incoming = draw_incoming(jax.random.fold_in(key_of[12], 71), 0)
    scene_lengths = jax.vmap(lambda own: ragged(own, SCENES, TOK, TOK // 2, 2))(jax.random.split(key_of[1], SEGMENTS)).reshape((SEGMENTS, SCENES)).astype(jnp.int32)
    attn_gain = jnp.clip(1.0 + 0.18 * jax.random.normal(key_of[2], (SEGMENTS, D), jnp.float32), 0.1, 1.9)
    query_weight = draw_query_weight(jax.random.fold_in(key_of[12], 71), 0)
    key_weight = draw_key_weight(jax.random.fold_in(key_of[12], 71), 0)
    value_weight = draw_value_weight(jax.random.fold_in(key_of[12], 71), 0)
    output_weight = draw_output_weight(jax.random.fold_in(key_of[12], 71), 0)
    ffn_gain = jnp.clip(1.0 + 0.18 * jax.random.normal(key_of[7], (SEGMENTS, D), jnp.float32), 0.1, 1.9)
    up_first = normal_values(key_of[8], (SEGMENTS, BLOCKS, BLOCK_IN, BLOCK_OUT), BLOCK_IN ** -0.5, 0.4375, ((0, 8), (1, 32)))
    up_second = normal_values(key_of[9], (SEGMENTS, BLOCKS, BLOCK_OUT, BLOCK_OUT), (BLOCK_OUT // 4) ** -0.5, 0.4375, ((0, 8), (1, 32)))
    down_first = normal_values(key_of[10], (SEGMENTS, BLOCKS, BLOCK_OUT, BLOCK_OUT), BLOCK_OUT ** -0.5, 0.21875, ((0, 8), (1, 32)))
    down_second = normal_values(key_of[11], (SEGMENTS, BLOCKS, BLOCK_OUT, BLOCK_IN), (BLOCK_OUT // 16) ** -0.5, 0.875, ((0, 8), (1, 32)))
    return {"incoming": incoming, "scene_lengths": scene_lengths, "attn_gain": attn_gain, "query_weight": query_weight, "key_weight": key_weight, "value_weight": value_weight, "output_weight": output_weight, "ffn_gain": ffn_gain, "up_first": up_first, "up_second": up_second, "down_first": down_first, "down_second": down_second}


epsilon = 1e-06

def norm_rows(values, gain):
    values_f = values.astype(jnp.float32)
    scaling = lax.rsqrt(lax.optimization_barrier(jnp.mean(values_f * values_f, axis=1, keepdims=True)) + epsilon)
    return (values_f * scaling * gain).astype(jnp.bfloat16)

def scene_mask(lengths_row):
    positions = jnp.arange(TOK, dtype=jnp.int32)
    bounds = jnp.cumsum(lengths_row.astype(jnp.int32))
    scene = lax.optimization_barrier(jnp.sum((positions[:, None] >= bounds[None, :]).astype(jnp.int32), axis=1))
    return scene[:, None] == scene[None, :]

def one_head(packed, allowed):
    query_head, key_head, value_head = packed
    scores = jnp.dot(query_head, key_head.T, preferred_element_type=jnp.float32) * HEAD ** (-0.5)
    scores = jnp.where(allowed, scores, -jnp.inf)
    peak = lax.optimization_barrier(jnp.max(scores, axis=1, keepdims=True))
    expo = jnp.exp(scores - peak)
    probs = (expo / lax.optimization_barrier(jnp.sum(expo, axis=1, keepdims=True))).astype(jnp.bfloat16)
    return jnp.dot(probs, value_head, preferred_element_type=jnp.float32).astype(jnp.bfloat16)

def split_heads(matrix):
    return matrix.reshape(TOK, HEADS, HEAD).transpose(1, 0, 2)

def segment_layer(received_cols, lengths_row, attn_gain, query_weight, key_weight, value_weight, output_weight, ffn_gain, up_first, up_second, down_first, down_second):
    received = received_cols.T
    allowed = scene_mask(lengths_row)
    normed = norm_rows(received, attn_gain)
    query = jnp.dot(normed, query_weight.T, preferred_element_type=jnp.float32).astype(jnp.bfloat16)
    keys = jnp.dot(normed, key_weight.T, preferred_element_type=jnp.float32).astype(jnp.bfloat16)
    values = jnp.dot(normed, value_weight.T, preferred_element_type=jnp.float32).astype(jnp.bfloat16)
    per_head = lax.map(lambda packed: one_head(packed, allowed), (split_heads(query), split_heads(keys), split_heads(values)))
    attended = per_head.transpose(1, 0, 2).reshape(TOK, D)
    group_width = GROUP_HEADS * HEAD

    def add_group(index, total):
        start = jnp.asarray(index, jnp.int32) * group_width
        columns = lax.dynamic_slice_in_dim(attended, start, group_width, 1)
        weight_rows = lax.dynamic_slice_in_dim(output_weight, start, group_width, 0)
        partial_sum = jnp.dot(columns, weight_rows, preferred_element_type=jnp.float32).astype(jnp.bfloat16)
        partial_sum = lax.optimization_barrier(partial_sum)
        return total + partial_sum.astype(jnp.float32)
    head_sum = lax.fori_loop(0, N_TENSOR, add_group, jnp.zeros((TOK, D), jnp.float32))
    middle = (received.astype(jnp.float32) + head_sum).astype(jnp.bfloat16)
    ffn_normed = norm_rows(middle, ffn_gain)
    spread = jnp.einsum('tif,ifkm->kimt', ffn_normed.reshape(TOK, BLOCKS, BLOCK_IN).astype(jnp.float32), up_first.reshape(BLOCKS, BLOCK_IN, BLOCKS, PIECE).astype(jnp.float32)).astype(jnp.bfloat16)
    hidden_pre = jnp.einsum('kimt,kimg->kgt', spread.astype(jnp.float32), up_second.reshape(BLOCKS, BLOCKS, PIECE, BLOCK_OUT).astype(jnp.float32))
    hidden = jax.nn.gelu(hidden_pre, approximate=True).astype(jnp.bfloat16)
    mixed_back = jnp.einsum('kgt,kgim->kimt', hidden.astype(jnp.float32), down_first.reshape(BLOCKS, BLOCK_OUT, BLOCKS, PIECE).astype(jnp.float32)).astype(jnp.bfloat16)
    ffn_out = jnp.einsum('kimt,ikmf->tif', mixed_back.astype(jnp.float32), down_second.reshape(BLOCKS, BLOCKS, PIECE, BLOCK_IN).astype(jnp.float32))
    produced = (middle.astype(jnp.float32) + ffn_out.reshape(TOK, D)).astype(jnp.bfloat16)
    return produced.T

def reference(incoming, scene_lengths, attn_gain, query_weight, key_weight, value_weight, output_weight, ffn_gain, up_first, up_second, down_first, down_second):
    stacked = incoming.reshape(D, SEGMENTS, TOK).transpose(1, 0, 2)
    received = jnp.roll(stacked, 1, axis=0)
    produced = lax.map(lambda packed: segment_layer(*packed), (received, scene_lengths, attn_gain, query_weight, key_weight, value_weight, output_weight, ffn_gain, up_first, up_second, down_first, down_second))
    return produced.transpose(1, 0, 2).reshape(D, SEGMENTS * TOK)
```

```python
import jax
import jax.numpy as jnp
from jax import lax
from jax.experimental import pallas as pl
from jax.experimental.pallas import tpu as pltpu
from jax.sharding import Mesh, PartitionSpec as P

D = 6144
HEAD = 192
TOK = 1024
BLOCKS = 32
PIECE = 24
WIDE = 768
CHUNK = 256
NX, NZ, NY = 4, 2, 4
EXTRA = 128

epsilon = 1e-06


def attend_kernel(place_ref, lengths_ref, gain_ref, wq_ref, wk_ref, wv_ref, g_ref, out_ref, acc_ref, squares_ref):
    step = pl.program_id(0)

    @pl.when(step == 0)
    def _():
        acc_ref[...] = jnp.zeros_like(acc_ref)
        squares_ref[...] = jnp.zeros_like(squares_ref)

    block = g_ref[...].reshape(NY * HEAD, TOK)
    block_f = block.astype(jnp.float32)
    squares_ref[...] += jnp.sum((block_f * block_f).reshape(NY * HEAD // 8, 8, TOK), axis=0)
    gain = gain_ref[...]
    weight = jnp.concatenate(
        [(ref[0].astype(jnp.float32) * gain).astype(jnp.bfloat16) for ref in (wq_ref, wk_ref, wv_ref)], axis=0
    )
    acc_ref[...] += jnp.dot(weight, block, preferred_element_type=jnp.float32)

    @pl.when(step == pl.num_programs(0) - 1)
    def _():
        total = jnp.sum(squares_ref[...], axis=0, keepdims=True)
        scaling = lax.rsqrt(total * (1.0 / D) + epsilon)
        query = (acc_ref[0:HEAD, :] * scaling).astype(jnp.bfloat16)
        keys = (acc_ref[HEAD : 2 * HEAD, :] * scaling).T.astype(jnp.bfloat16)
        values = (acc_ref[2 * HEAD :, :] * scaling).astype(jnp.bfloat16)
        first = lengths_ref[0, 0]
        second = first + lengths_ref[0, 1]
        third = second + lengths_ref[0, 2]

        def scene(position):
            return (
                (position >= first).astype(jnp.int32)
                + (position >= second).astype(jnp.int32)
                + (position >= third).astype(jnp.int32)
            )

        key_scene = scene(lax.broadcasted_iota(jnp.int32, (TOK, 1), 0))
        for part in range(TOK // CHUNK):
            cols = slice(part * CHUNK, (part + 1) * CHUNK)
            query_scene = scene(lax.broadcasted_iota(jnp.int32, (1, CHUNK), 1) + part * CHUNK)
            scores = jnp.dot(keys, query[:, cols], preferred_element_type=jnp.float32)
            scores = jnp.where(key_scene == query_scene, scores * HEAD ** (-0.5), -jnp.inf)
            expo = jnp.exp(scores - jnp.max(scores, axis=0, keepdims=True))
            weight_sum = jnp.sum(expo, axis=0, keepdims=True)
            mixed = jnp.dot(values, expo.astype(jnp.bfloat16), preferred_element_type=jnp.float32)
            mixed = (mixed / weight_sum).astype(jnp.bfloat16)
            for peer in range(NZ * NY):
                out_ref[peer, :, cols] = mixed


def attention(place, lengths, gain, query_weight, key_weight, value_weight, gathered):
    steps = NX * NZ

    def weight_map(k, place_ref):
        return (0, 0, 2 * (k // 2) + (k % 2 + place_ref[0]) % 2)

    weight_spec = pl.BlockSpec((1, HEAD, NY * HEAD), weight_map)
    return pl.pallas_call(
        attend_kernel,
        grid_spec=pltpu.PrefetchScalarGridSpec(
            num_scalar_prefetch=1,
            grid=(steps,),
            in_specs=[
                pl.BlockSpec(memory_space=pltpu.SMEM),
                pl.BlockSpec((1, NY * HEAD), lambda k, place_ref: weight_map(k, place_ref)[1:]),
                weight_spec,
                weight_spec,
                weight_spec,
                pl.BlockSpec((1, NY, 1, HEAD, TOK), lambda k, place_ref: (k // 2, 0, k % 2, 0, 0)),
            ],
            out_specs=pl.BlockSpec((NZ * NY, HEAD, TOK), lambda k, place_ref: (0, 0, 0)),
            scratch_shapes=[pltpu.VMEM((3 * HEAD, TOK), jnp.float32), pltpu.VMEM((8, TOK), jnp.float32)],
        ),
        out_shape=jax.ShapeDtypeStruct((NZ * NY, HEAD, TOK), jnp.bfloat16),
        compiler_params=pltpu.CompilerParams(vmem_limit_bytes=48 * 1024 * 1024),
        cost_estimate=pl.CostEstimate(flops=8_000_000_000, bytes_accessed=22_000_000, transcendentals=1_000_000),
        name="attention",
    )(place, lengths, gain, query_weight, key_weight, value_weight, gathered)


def project_kernel(w_ref, a_ref, out_ref):
    out_ref[...] = jnp.dot(w_ref[...], a_ref[...], preferred_element_type=jnp.float32).astype(jnp.bfloat16)


def project(weight, attended):
    return pl.pallas_call(
        project_kernel,
        grid=(TOK // CHUNK,),
        in_specs=[
            pl.BlockSpec((WIDE, NZ * NY * HEAD), lambda k: (0, 0)),
            pl.BlockSpec((NZ * NY * HEAD, CHUNK), lambda k: (0, k)),
        ],
        out_specs=pl.BlockSpec((WIDE, CHUNK), lambda k: (0, k)),
        out_shape=jax.ShapeDtypeStruct((WIDE, TOK), jnp.bfloat16),
        compiler_params=pltpu.CompilerParams(vmem_limit_bytes=40 * 1024 * 1024),
        cost_estimate=pl.CostEstimate(flops=2_500_000_000, bytes_accessed=7_000_000, transcendentals=0),
        name="project",
    )(weight, attended)


def spread_kernel(parts_ref, received_ref, gain_ref, up_ref, middle_ref, out_ref):
    total = received_ref[...].astype(jnp.float32)
    head_sum = parts_ref[0].astype(jnp.float32)
    for x in range(1, NX):
        head_sum += parts_ref[x].astype(jnp.float32)
    middle = (total + head_sum).astype(jnp.bfloat16)
    middle_ref[...] = middle
    middle_f = middle.astype(jnp.float32)
    squares = jnp.sum(middle_f * middle_f, axis=0, keepdims=True)
    high = squares.astype(jnp.bfloat16).astype(jnp.float32)
    low = squares - high
    rows = [high[:, k * 128 : (k + 1) * 128] for k in range(8)] + [low[:, k * 128 : (k + 1) * 128] for k in range(8)]
    tile = jnp.concatenate(rows + [jnp.zeros((8, 128), jnp.float32)], axis=0)
    out_ref[:, TOK:] = jnp.concatenate([tile] * BLOCKS, axis=0).astype(jnp.bfloat16)
    scaled = (middle_f * gain_ref[...]).astype(jnp.bfloat16)
    out_ref[:, :TOK] = jnp.dot(up_ref[...], scaled, preferred_element_type=jnp.float32).astype(jnp.bfloat16)


def spread_call(parts, received, gain, up):
    return pl.pallas_call(
        spread_kernel,
        out_shape=(
            jax.ShapeDtypeStruct((HEAD, TOK), jnp.bfloat16),
            jax.ShapeDtypeStruct((WIDE, TOK + EXTRA), jnp.bfloat16),
        ),
        compiler_params=pltpu.CompilerParams(vmem_limit_bytes=40 * 1024 * 1024),
        cost_estimate=pl.CostEstimate(flops=310_000_000, bytes_accessed=5_000_000, transcendentals=0),
        name="spread",
    )(parts, received, gain, up)


def hidden_kernel(up_ref, down_ref, r_ref, out_ref):
    sums = jnp.sum(r_ref[:, TOK:].astype(jnp.float32).reshape(BLOCKS, PIECE, 128), axis=0)
    sums = sums[0:8] + sums[8:16]
    total = jnp.concatenate([sums[k : k + 1] for k in range(8)], axis=1)
    scaling = lax.rsqrt(total * (1.0 / D) + epsilon)
    for part in range(TOK // CHUNK):
        cols = slice(part * CHUNK, (part + 1) * CHUNK)
        pre = jnp.dot(up_ref[...], r_ref[:, cols], preferred_element_type=jnp.float32) * scaling[:, cols]
        hidden = 0.5 * pre * (1.0 + jnp.tanh(0.7978845608028654 * (pre + 0.044715 * (pre * pre * pre))))
        out_ref[:, cols] = jnp.dot(
            down_ref[...], hidden.astype(jnp.bfloat16), preferred_element_type=jnp.float32
        ).astype(jnp.bfloat16)


def hidden_call(up, down, pieces):
    return pl.pallas_call(
        hidden_kernel,
        out_shape=jax.ShapeDtypeStruct((WIDE, TOK), jnp.bfloat16),
        compiler_params=pltpu.CompilerParams(vmem_limit_bytes=40 * 1024 * 1024),
        cost_estimate=pl.CostEstimate(flops=2_500_000_000, bytes_accessed=6_000_000, transcendentals=1_000_000),
        name="hidden",
    )(up, down, pieces)


def final_kernel(down_ref, b_ref, middle_ref, out_ref):
    out = jnp.dot(down_ref[...], b_ref[...], preferred_element_type=jnp.float32)
    out_ref[...] = (middle_ref[...].astype(jnp.float32) + out).astype(jnp.bfloat16)


def final_call(down, pieces, middle):
    return pl.pallas_call(
        final_kernel,
        out_shape=jax.ShapeDtypeStruct((HEAD, TOK), jnp.bfloat16),
        compiler_params=pltpu.CompilerParams(vmem_limit_bytes=40 * 1024 * 1024),
        cost_estimate=pl.CostEstimate(flops=310_000_000, bytes_accessed=3_000_000, transcendentals=0),
        name="final",
    )(down, pieces, middle)


TENSOR = ("x", "z", "y")


def shift_pairs(count, flip):
    pairs = []
    for s in range(count):
        for x in range(NX):
            for z in range(NZ):
                for y in range(NY):
                    source = ((s * NX + x) * NZ + z) * NY + y
                    target = ((((s + 1) % count) * NX + x) * NZ + (z ^ flip)) * NY + y
                    pairs.append((source, target))
    return pairs


def shards(
    incoming,
    scene_lengths,
    attn_gain,
    query_weight,
    key_weight,
    value_weight,
    output_weight,
    ffn_gain,
    up_first,
    up_second,
    down_first,
    down_second,
):
    everything = ("pipe",) + TENSOR
    count = lax.axis_size("pipe")
    received = lax.ppermute(incoming, everything, shift_pairs(count, 0))
    beside = lax.ppermute(incoming, everything, shift_pairs(count, 1))
    pair = jnp.concatenate([received, beside], axis=0)
    gathered = lax.all_gather(pair, ("x", "y"), axis=0, tiled=True)

    tied = lax.optimization_barrier((pair, output_weight, up_first, up_second, down_first, down_second))
    _, output_weight, up_first, up_second, down_first, down_second = tied
    blocks = output_weight.reshape(HEAD, NX, NZ * NY, HEAD).transpose(2, 0, 1, 3).reshape(NZ * NY, HEAD, WIDE)
    blocks = lax.all_to_all(blocks, ("z", "y"), split_axis=0, concat_axis=0, tiled=True)
    out_weight = blocks.reshape(NZ * NY * HEAD, WIDE).T
    up_first = up_first.reshape(HEAD, WIDE).T
    up_second = up_second.reshape(WIDE, WIDE).T
    down_first = down_first.reshape(WIDE, WIDE).T
    down_second = down_second.reshape(WIDE, HEAD).T
    gathered, out_weight, up_first, up_second, down_first, down_second = lax.optimization_barrier(
        (gathered, out_weight, up_first, up_second, down_first, down_second)
    )

    place = lax.axis_index("z").astype(jnp.int32).reshape(1)
    attended = attention(
        place,
        scene_lengths,
        attn_gain,
        query_weight,
        key_weight,
        value_weight,
        gathered.reshape(NX, NY, NZ, HEAD, TOK),
    )
    group = lax.all_to_all(attended, ("z", "y"), split_axis=0, concat_axis=0, tiled=True)
    partial = project(out_weight, group.reshape(NZ * NY * HEAD, TOK))
    parts = lax.all_to_all(partial.reshape(NX, HEAD, TOK), "x", split_axis=0, concat_axis=0, tiled=True)
    middle, spread = spread_call(parts, received, ffn_gain.reshape(HEAD, 1), up_first)
    pieces = lax.all_to_all(
        spread.reshape(BLOCKS, PIECE, TOK + EXTRA), TENSOR, split_axis=0, concat_axis=0, tiled=True
    )
    mixed_back = hidden_call(up_second, down_first, pieces.reshape(WIDE, TOK + EXTRA))
    returned = lax.all_to_all(
        mixed_back.reshape(BLOCKS, PIECE, TOK), TENSOR, split_axis=0, concat_axis=0, tiled=True
    )
    return final_call(down_second, returned.reshape(WIDE, TOK), middle)


def solution(mesh):
    devices = mesh.devices
    finer = Mesh(devices.reshape(devices.shape[0], NX, NZ, NY), ("pipe",) + TENSOR)
    return jax.shard_map(
        shards,
        mesh=finer,
        in_specs=(
            P(TENSOR, "pipe"),
            P("pipe", None),
            P("pipe", None),
            P("pipe", TENSOR, None),
            P("pipe", TENSOR, None),
            P("pipe", TENSOR, None),
            P("pipe", TENSOR, None),
            P("pipe", TENSOR),
            P("pipe", TENSOR, None, None),
            P("pipe", TENSOR, None, None),
            P("pipe", TENSOR, None, None),
            P("pipe", TENSOR, None, None),
        ),
        out_specs=P(TENSOR, "pipe"),
        check_vma=False,
    )
```

```python
import functools

import jax
import jax.numpy as jnp
from jax import lax
from jax.experimental import pallas as pl
from jax.experimental.pallas import tpu as pltpu
from jax.sharding import Mesh, PartitionSpec as P

D = 6144
HEAD = 192
TOK = 1024
BLOCKS = 32
PIECE = 24
WIDE = 768
CHUNK = 256
NX, NZ, NY = 4, 2, 4
EXTRA = 128

epsilon = 1e-06


def scale_kernel(half_ref, gain_ref, wq_ref, wk_ref, wv_ref, out_ref):
    gain = gain_ref[...]
    for part, ref in enumerate((wq_ref, wk_ref, wv_ref)):
        out_ref[0, part * HEAD : (part + 1) * HEAD, :] = (ref[0].astype(jnp.float32) * gain).astype(jnp.bfloat16)


def half_weights(half, gain, query_weight, key_weight, value_weight):
    weight_spec = pl.BlockSpec((1, HEAD, WIDE), lambda k, half_ref: (0, 0, 2 * k + half_ref[0]))
    return pl.pallas_call(
        scale_kernel,
        grid_spec=pltpu.PrefetchScalarGridSpec(
            num_scalar_prefetch=1,
            grid=(NX,),
            in_specs=[
                pl.BlockSpec((1, WIDE), lambda k, half_ref: (0, 2 * k + half_ref[0])),
                weight_spec,
                weight_spec,
                weight_spec,
            ],
            out_specs=pl.BlockSpec((1, 3 * HEAD, WIDE), lambda k, half_ref: (k, 0, 0)),
        ),
        out_shape=jax.ShapeDtypeStruct((NX, 3 * HEAD, WIDE), jnp.bfloat16),
        compiler_params=pltpu.CompilerParams(vmem_limit_bytes=58 * 1024 * 1024),
        cost_estimate=pl.CostEstimate(flops=0, bytes_accessed=7_000_000, transcendentals=0),
        name="half_weights",
    )(half, gain, query_weight, key_weight, value_weight)


def accumulate(product, acc_ref):
    @pl.when(pl.program_id(0) == 0)
    def _():
        acc_ref[...] = product

    @pl.when(pl.program_id(0) > 0)
    def _():
        acc_ref[...] += product


def cross_kernel(w_ref, g_ref, squares_ref, out_ref, values_ref, acc_ref):
    accumulate(jnp.dot(w_ref[0], g_ref[0], preferred_element_type=jnp.float32), acc_ref)

    @pl.when(pl.program_id(0) == pl.num_programs(0) - 1)
    def _():
        out_ref[: 2 * HEAD, :] = acc_ref[: 2 * HEAD, :].astype(jnp.bfloat16)
        values_ref[...] = acc_ref[2 * HEAD :, :].astype(jnp.bfloat16)
        total = jnp.sum(squares_ref[...], axis=0, keepdims=True)
        high = total.astype(jnp.bfloat16).astype(jnp.float32)
        tail = jnp.concatenate([high, total - high, jnp.zeros((14, TOK), jnp.float32)], axis=0)
        out_ref[2 * HEAD :, :] = tail.astype(jnp.bfloat16)


def cross_projection(weights, gathered, squares):
    return pl.pallas_call(
        cross_kernel,
        grid=(NX,),
        in_specs=[
            pl.BlockSpec((1, 3 * HEAD, WIDE), lambda k: (k, 0, 0)),
            pl.BlockSpec((1, WIDE, TOK), lambda k: (k, 0, 0)),
            pl.BlockSpec((8, TOK), lambda k: (0, 0)),
        ],
        out_specs=(
            pl.BlockSpec((2 * HEAD + 16, TOK), lambda k: (0, 0)),
            pl.BlockSpec((HEAD, TOK), lambda k: (0, 0)),
        ),
        out_shape=(
            jax.ShapeDtypeStruct((2 * HEAD + 16, TOK), jnp.bfloat16),
            jax.ShapeDtypeStruct((HEAD, TOK), jnp.bfloat16),
        ),
        scratch_shapes=[pltpu.VMEM((3 * HEAD, TOK), jnp.float32)],
        compiler_params=pltpu.CompilerParams(vmem_limit_bytes=58 * 1024 * 1024),
        cost_estimate=pl.CostEstimate(flops=3_600_000_000, bytes_accessed=10_000_000, transcendentals=0),
        name="cross_projection",
    )(weights, gathered, squares)


def own_kernel(place_ref, gain_ref, wq_ref, wk_ref, wv_ref, g_ref, out_ref, squares_ref):
    gain = gain_ref[...]
    weight = jnp.concatenate(
        [(ref[0].astype(jnp.float32) * gain).astype(jnp.bfloat16) for ref in (wq_ref, wk_ref, wv_ref)], axis=0
    )
    accumulate(jnp.dot(weight, g_ref[0], preferred_element_type=jnp.float32), out_ref)
    block = g_ref[0].astype(jnp.float32)
    accumulate(jnp.sum((block * block).reshape(WIDE // 8, 8, TOK), axis=0), squares_ref)


def own_projection(place, gain, query_weight, key_weight, value_weight, gathered):
    weight_spec = pl.BlockSpec((1, HEAD, WIDE), lambda k, place_ref: (0, 0, 2 * k + place_ref[0]))
    return pl.pallas_call(
        own_kernel,
        grid_spec=pltpu.PrefetchScalarGridSpec(
            num_scalar_prefetch=1,
            grid=(NX,),
            in_specs=[
                pl.BlockSpec((1, WIDE), lambda k, place_ref: (0, 2 * k + place_ref[0])),
                weight_spec,
                weight_spec,
                weight_spec,
                pl.BlockSpec((1, WIDE, TOK), lambda k, place_ref: (k, 0, 0)),
            ],
            out_specs=(
                pl.BlockSpec((3 * HEAD, TOK), lambda k, place_ref: (0, 0)),
                pl.BlockSpec((8, TOK), lambda k, place_ref: (0, 0)),
            ),
        ),
        out_shape=(
            jax.ShapeDtypeStruct((3 * HEAD, TOK), jnp.float32),
            jax.ShapeDtypeStruct((8, TOK), jnp.float32),
        ),
        compiler_params=pltpu.CompilerParams(vmem_limit_bytes=58 * 1024 * 1024),
        cost_estimate=pl.CostEstimate(flops=1_000_000, bytes_accessed=10_000, transcendentals=0),
        name="own_projection",
    )(place, gain, query_weight, key_weight, value_weight, gathered)


def scaling_of(squares_ref, tail):
    tail = tail.astype(jnp.float32)
    total = jnp.sum(squares_ref[...], axis=0, keepdims=True) + tail[0:1] + tail[1:2]
    return lax.rsqrt(total * (1.0 / D) + epsilon)


def weigh_kernel(lengths_ref, own_ref, came_ref, squares_ref, expo_ref, rows_ref):
    scaling = scaling_of(squares_ref, came_ref[2 * HEAD :, :])
    both = (own_ref[: 2 * HEAD, :] + came_ref[: 2 * HEAD, :].astype(jnp.float32)) * scaling
    query = both[:HEAD, :].astype(jnp.bfloat16)
    keys = both[HEAD:, :].astype(jnp.bfloat16).T
    rows_ref[0:1, :] = scaling
    first = lengths_ref[0, 0]
    second = first + lengths_ref[0, 1]
    third = second + lengths_ref[0, 2]

    def scene(position):
        return (
            (position >= first).astype(jnp.int32)
            + (position >= second).astype(jnp.int32)
            + (position >= third).astype(jnp.int32)
        )

    key_scene = scene(lax.broadcasted_iota(jnp.int32, (TOK, 1), 0))
    for part in range(TOK // CHUNK):
        cols = slice(part * CHUNK, (part + 1) * CHUNK)
        query_scene = scene(lax.broadcasted_iota(jnp.int32, (1, CHUNK), 1) + part * CHUNK)
        scores = jnp.dot(keys, query[:, cols], preferred_element_type=jnp.float32)
        scores = jnp.where(key_scene == query_scene, scores * HEAD ** (-0.5), -jnp.inf)
        expo = jnp.exp(scores - jnp.max(scores, axis=0, keepdims=True))
        rows_ref[1:2, cols] = 1.0 / jnp.sum(expo, axis=0, keepdims=True)
        expo_ref[:, cols] = expo.astype(jnp.bfloat16)


def attention_weights(lengths, own, came, squares):
    whole = pl.BlockSpec(memory_space=pltpu.VMEM)
    return pl.pallas_call(
        weigh_kernel,
        in_specs=[pl.BlockSpec(memory_space=pltpu.SMEM)] + [whole] * 3,
        out_shape=(
            jax.ShapeDtypeStruct((TOK, TOK), jnp.bfloat16),
            jax.ShapeDtypeStruct((2, TOK), jnp.float32),
        ),
        compiler_params=pltpu.CompilerParams(vmem_limit_bytes=24 * 1024 * 1024),
        cost_estimate=pl.CostEstimate(flops=500_000_000, bytes_accessed=6_000_000, transcendentals=1_000_000),
        name="attention_weights",
    )(lengths, own, came, squares)


def mix_kernel(own_ref, came_ref, expo_ref, rows_ref, out_ref):
    values = (own_ref[2 * HEAD :, :] + came_ref[...].astype(jnp.float32)) * rows_ref[0:1, :]
    values = values.astype(jnp.bfloat16)
    for part in range(TOK // CHUNK):
        cols = slice(part * CHUNK, (part + 1) * CHUNK)
        mixed = jnp.dot(values, expo_ref[:, cols], preferred_element_type=jnp.float32)
        mixed = (mixed * rows_ref[1:2, cols]).astype(jnp.bfloat16)
        for peer in range(NX):
            out_ref[peer, :, cols] = mixed


def mix_values(own, came, expo, rows):
    return pl.pallas_call(
        mix_kernel,
        out_shape=jax.ShapeDtypeStruct((NX, HEAD, TOK), jnp.bfloat16),
        compiler_params=pltpu.CompilerParams(vmem_limit_bytes=20 * 1024 * 1024),
        cost_estimate=pl.CostEstimate(flops=400_000_000, bytes_accessed=7_000_000, transcendentals=0),
        name="mix_values",
    )(own, came, expo, rows)


def copy_kernel(in_ref, out_ref):
    out_ref[...] = in_ref[...]


def slice_columns(weight):
    width = NZ * NY * HEAD
    return pl.pallas_call(
        copy_kernel,
        grid=(NX,),
        in_specs=[pl.BlockSpec((1, HEAD, width), lambda k: (0, 0, k))],
        out_specs=pl.BlockSpec((1, HEAD, width), lambda k: (k, 0, 0)),
        out_shape=jax.ShapeDtypeStruct((NX, HEAD, width), jnp.bfloat16),
        compiler_params=pltpu.CompilerParams(vmem_limit_bytes=48 * 1024 * 1024),
        cost_estimate=pl.CostEstimate(flops=0, bytes_accessed=5_000_000, transcendentals=0),
        name="slice_columns",
    )(weight)


def project_kernel(w_ref, a_ref, out_ref):
    out_ref[...] = jnp.dot(w_ref[...], a_ref[...], preferred_element_type=jnp.float32).astype(jnp.bfloat16)


def project(weight, attended):
    return pl.pallas_call(
        project_kernel,
        grid=(TOK // CHUNK,),
        in_specs=[
            pl.BlockSpec((NZ * NY * HEAD, NX * HEAD), lambda k: (0, 0)),
            pl.BlockSpec((NX * HEAD, CHUNK), lambda k: (0, k)),
        ],
        out_specs=pl.BlockSpec((NZ * NY * HEAD, CHUNK), lambda k: (0, k)),
        out_shape=jax.ShapeDtypeStruct((NZ * NY * HEAD, TOK), jnp.bfloat16),
        compiler_params=pltpu.CompilerParams(vmem_limit_bytes=24 * 1024 * 1024),
        cost_estimate=pl.CostEstimate(flops=2_500_000_000, bytes_accessed=7_000_000, transcendentals=0),
        name="project",
    )(weight, attended)


def spread_kernel(parts_ref, received_ref, gain_ref, up_ref, middle_ref, out_ref):
    total = received_ref[...].astype(jnp.float32)
    head_sum = parts_ref[0].astype(jnp.float32)
    for x in range(1, NZ * NY):
        head_sum += parts_ref[x].astype(jnp.float32)
    middle = (total + head_sum).astype(jnp.bfloat16)
    middle_ref[...] = middle
    middle_f = middle.astype(jnp.float32)
    squares = jnp.sum(middle_f * middle_f, axis=0, keepdims=True)
    high = squares.astype(jnp.bfloat16).astype(jnp.float32)
    low = squares - high
    rows = [high[:, k * 128 : (k + 1) * 128] for k in range(8)] + [low[:, k * 128 : (k + 1) * 128] for k in range(8)]
    tile = jnp.concatenate(rows + [jnp.zeros((8, 128), jnp.float32)], axis=0)
    out_ref[:, TOK:] = jnp.concatenate([tile] * BLOCKS, axis=0).astype(jnp.bfloat16)
    scaled = (middle_f * gain_ref[...]).astype(jnp.bfloat16)
    out_ref[:, :TOK] = jnp.dot(up_ref[...], scaled, preferred_element_type=jnp.float32).astype(jnp.bfloat16)


def spread_call(parts, received, gain, up):
    return pl.pallas_call(
        spread_kernel,
        out_shape=(
            jax.ShapeDtypeStruct((HEAD, TOK), jnp.bfloat16),
            jax.ShapeDtypeStruct((WIDE, TOK + EXTRA), jnp.bfloat16),
        ),
        compiler_params=pltpu.CompilerParams(vmem_limit_bytes=20 * 1024 * 1024),
        cost_estimate=pl.CostEstimate(flops=310_000_000, bytes_accessed=5_000_000, transcendentals=0),
        name="spread",
    )(parts, received, gain, up)


def hidden_kernel(up_ref, down_ref, r_ref, out_ref):
    sums = jnp.sum(r_ref[:, TOK:].astype(jnp.float32).reshape(BLOCKS, PIECE, 128), axis=0)
    sums = sums[0:8] + sums[8:16]
    total = jnp.concatenate([sums[k : k + 1] for k in range(8)], axis=1)
    scaling = lax.rsqrt(total * (1.0 / D) + epsilon)
    for part in range(TOK // CHUNK):
        cols = slice(part * CHUNK, (part + 1) * CHUNK)
        pre = jnp.dot(up_ref[...], r_ref[:, cols], preferred_element_type=jnp.float32) * scaling[:, cols]
        hidden = 0.5 * pre * (1.0 + jnp.tanh(0.7978845608028654 * (pre + 0.044715 * (pre * pre * pre))))
        out_ref[:, cols] = jnp.dot(
            down_ref[...], hidden.astype(jnp.bfloat16), preferred_element_type=jnp.float32
        ).astype(jnp.bfloat16)


def hidden_call(up, down, pieces):
    return pl.pallas_call(
        hidden_kernel,
        out_shape=jax.ShapeDtypeStruct((WIDE, TOK), jnp.bfloat16),
        compiler_params=pltpu.CompilerParams(vmem_limit_bytes=24 * 1024 * 1024),
        cost_estimate=pl.CostEstimate(flops=2_500_000_000, bytes_accessed=6_000_000, transcendentals=1_000_000),
        name="hidden",
    )(up, down, pieces)


def final_kernel(down_ref, b_ref, middle_ref, out_ref):
    out = jnp.dot(down_ref[...], b_ref[...], preferred_element_type=jnp.float32)
    out_ref[...] = (middle_ref[...].astype(jnp.float32) + out).astype(jnp.bfloat16)


def final_call(down, pieces, middle):
    return pl.pallas_call(
        final_kernel,
        out_shape=jax.ShapeDtypeStruct((HEAD, TOK), jnp.bfloat16),
        compiler_params=pltpu.CompilerParams(vmem_limit_bytes=16 * 1024 * 1024),
        cost_estimate=pl.CostEstimate(flops=310_000_000, bytes_accessed=3_000_000, transcendentals=0),
        name="final",
    )(down, pieces, middle)


TENSOR = ("x", "z", "y")


def shift_pairs(count):
    devices = NX * NZ * NY
    return [(t, (t + devices) % (count * devices)) for t in range(count * devices)]


SWAP = [(0, 1), (1, 0)]


def shards(
    incoming,
    scene_lengths,
    attn_gain,
    query_weight,
    key_weight,
    value_weight,
    output_weight,
    ffn_gain,
    up_first,
    up_second,
    down_first,
    down_second,
):
    everything = ("pipe",) + TENSOR
    count = lax.axis_size("pipe")
    received = lax.ppermute(incoming, everything, shift_pairs(count))
    place = lax.axis_index("z").astype(jnp.int32).reshape(1)
    beside = half_weights(1 - place, attn_gain, query_weight, key_weight, value_weight)
    columns = slice_columns(output_weight)
    ahead, _ = lax.optimization_barrier((received, beside))
    beside = lax.ppermute(beside, "z", SWAP)
    gathered = lax.all_gather(ahead, ("x", "y"), axis=0, tiled=True).reshape(NX, NY * HEAD, TOK)

    own, squares = own_projection(place, attn_gain, query_weight, key_weight, value_weight, gathered)
    beside, own, squares = lax.optimization_barrier((beside, own, squares))
    crossed, crossed_values = cross_projection(beside, gathered, squares)
    came = lax.ppermute(crossed, "z", SWAP)
    came_values = lax.ppermute(crossed_values, "z", SWAP)

    tied = (crossed, up_first, up_second, down_first, down_second, ffn_gain)
    _, up_first, up_second, down_first, down_second, ffn_gain = lax.optimization_barrier(tied)
    up_first = up_first.reshape(HEAD, WIDE).T
    up_second = up_second.reshape(WIDE, WIDE).T
    down_first = down_first.reshape(WIDE, WIDE).T
    down_second = down_second.reshape(WIDE, HEAD).T
    ffn_gain = ffn_gain.reshape(HEAD, 1)
    columns, up_first = lax.optimization_barrier((columns, up_first))
    blocks = lax.all_to_all(columns, "x", split_axis=0, concat_axis=0, tiled=True)
    out_weight = blocks.reshape(NX * HEAD, NZ * NY * HEAD).T
    tied = (came, up_first, up_second, down_first, down_second, ffn_gain)
    came, up_first, up_second, down_first, down_second, ffn_gain = lax.optimization_barrier(tied)
    expo, rows = attention_weights(scene_lengths, own, came, squares)
    attended = mix_values(own, came_values, expo, rows)
    group = lax.all_to_all(attended, "x", split_axis=0, concat_axis=0, tiled=True)
    partial = project(out_weight, group.reshape(NX * HEAD, TOK))
    parts = lax.all_to_all(
        partial.reshape(NZ * NY, HEAD, TOK), ("z", "y"), split_axis=0, concat_axis=0, tiled=True
    )
    middle, spread = spread_call(parts, received, ffn_gain, up_first)
    pieces = lax.all_to_all(
        spread.reshape(BLOCKS, PIECE, TOK + EXTRA), TENSOR, split_axis=0, concat_axis=0, tiled=True
    )
    mixed_back = hidden_call(up_second, down_first, pieces.reshape(WIDE, TOK + EXTRA))
    returned = lax.all_to_all(
        mixed_back.reshape(BLOCKS, PIECE, TOK), TENSOR, split_axis=0, concat_axis=0, tiled=True
    )
    return final_call(down_second, returned.reshape(WIDE, TOK), middle)


def solution(mesh):
    devices = mesh.devices
    finer = Mesh(devices.reshape(devices.shape[0], NX, NZ, NY), ("pipe",) + TENSOR)
    return jax.shard_map(
        shards,
        mesh=finer,
        in_specs=(
            P(TENSOR, "pipe"),
            P("pipe", None),
            P("pipe", None),
            P("pipe", TENSOR, None),
            P("pipe", TENSOR, None),
            P("pipe", TENSOR, None),
            P("pipe", TENSOR, None),
            P("pipe", TENSOR),
            P("pipe", TENSOR, None, None),
            P("pipe", TENSOR, None, None),
            P("pipe", TENSOR, None, None),
            P("pipe", TENSOR, None, None),
        ),
        out_specs=P(TENSOR, "pipe"),
        check_vma=False,
    )
```

```python
import functools

import jax
import jax.numpy as jnp
from jax import lax
from jax.experimental import pallas as pl
from jax.experimental.pallas import tpu as pltpu
from jax.sharding import Mesh, PartitionSpec as P

D = 6144
HEAD = 192
TOK = 1024
BLOCKS = 32
PIECE = 24
WIDE = 768
CHUNK = 256
NX, NZ, NY = 4, 2, 4
EXTRA = 128
MARK_FLOPS = 90_500_000_000

epsilon = 1e-06


def scale_kernel(half_ref, gain_ref, wq_ref, wk_ref, wv_ref, out_ref):
    gain = gain_ref[...]
    for part, ref in enumerate((wq_ref, wk_ref, wv_ref)):
        out_ref[0, part * HEAD : (part + 1) * HEAD, :] = (ref[0].astype(jnp.float32) * gain).astype(jnp.bfloat16)


def half_weights(half, gain, query_weight, key_weight, value_weight):
    weight_spec = pl.BlockSpec((1, HEAD, WIDE), lambda k, half_ref: (0, 0, 2 * k + half_ref[0]))
    return pl.pallas_call(
        scale_kernel,
        grid_spec=pltpu.PrefetchScalarGridSpec(
            num_scalar_prefetch=1,
            grid=(NX,),
            in_specs=[
                pl.BlockSpec((1, WIDE), lambda k, half_ref: (0, 2 * k + half_ref[0])),
                weight_spec,
                weight_spec,
                weight_spec,
            ],
            out_specs=pl.BlockSpec((1, 3 * HEAD, WIDE), lambda k, half_ref: (k, 0, 0)),
        ),
        out_shape=jax.ShapeDtypeStruct((NX, 3 * HEAD, WIDE), jnp.bfloat16),
        compiler_params=pltpu.CompilerParams(vmem_limit_bytes=58 * 1024 * 1024),
        cost_estimate=pl.CostEstimate(flops=0, bytes_accessed=7_000_000, transcendentals=0),
        name="half_weights",
    )(half, gain, query_weight, key_weight, value_weight)


def accumulate(product, acc_ref):
    @pl.when(pl.program_id(0) == 0)
    def _():
        acc_ref[...] = product

    @pl.when(pl.program_id(0) > 0)
    def _():
        acc_ref[...] += product


def cross_kernel(w_ref, g_ref, mark_ref, out_ref, values_ref, squares_ref, acc_ref):
    accumulate(jnp.dot(w_ref[0], g_ref[0], preferred_element_type=jnp.float32), acc_ref)
    block = g_ref[0].astype(jnp.float32)
    accumulate(jnp.sum((block * block).reshape(WIDE // 8, 8, TOK), axis=0), squares_ref)

    @pl.when(pl.program_id(0) == pl.num_programs(0) - 1)
    def _():
        out_ref[: 2 * HEAD, :] = acc_ref[: 2 * HEAD, :].astype(jnp.bfloat16)
        values_ref[...] = acc_ref[2 * HEAD :, :].astype(jnp.bfloat16)
        total = jnp.sum(squares_ref[...], axis=0, keepdims=True)
        high = total.astype(jnp.bfloat16).astype(jnp.float32)
        tail = jnp.concatenate([high, total - high, jnp.zeros((14, TOK), jnp.float32)], axis=0)
        out_ref[2 * HEAD :, :] = tail.astype(jnp.bfloat16)


def cross_projection(weights, gathered, mark):
    return pl.pallas_call(
        cross_kernel,
        grid=(NX,),
        in_specs=[
            pl.BlockSpec((1, 3 * HEAD, WIDE), lambda k: (k, 0, 0)),
            pl.BlockSpec((1, WIDE, TOK), lambda k: (k, 0, 0)),
            pl.BlockSpec(memory_space=pl.ANY),
        ],
        out_specs=(
            pl.BlockSpec((2 * HEAD + 16, TOK), lambda k: (0, 0)),
            pl.BlockSpec((HEAD, TOK), lambda k: (0, 0)),
            pl.BlockSpec((8, TOK), lambda k: (0, 0)),
        ),
        out_shape=(
            jax.ShapeDtypeStruct((2 * HEAD + 16, TOK), jnp.bfloat16),
            jax.ShapeDtypeStruct((HEAD, TOK), jnp.bfloat16),
            jax.ShapeDtypeStruct((8, TOK), jnp.float32),
        ),
        scratch_shapes=[pltpu.VMEM((3 * HEAD, TOK), jnp.float32)],
        compiler_params=pltpu.CompilerParams(vmem_limit_bytes=58 * 1024 * 1024),
        cost_estimate=pl.CostEstimate(flops=1_000_000, bytes_accessed=10_000, transcendentals=0),
        name="cross_projection",
    )(weights, gathered, mark)


def own_kernel(w_ref, g_ref, out_ref):
    accumulate(jnp.dot(w_ref[0], g_ref[0], preferred_element_type=jnp.float32), out_ref)


def own_projection(weights, gathered):
    return pl.pallas_call(
        own_kernel,
        grid=(NX,),
        in_specs=[
            pl.BlockSpec((1, 3 * HEAD, WIDE), lambda k: (k, 0, 0)),
            pl.BlockSpec((1, WIDE, TOK), lambda k: (k, 0, 0)),
        ],
        out_specs=pl.BlockSpec((3 * HEAD, TOK), lambda k: (0, 0)),
        out_shape=jax.ShapeDtypeStruct((3 * HEAD, TOK), jnp.float32),
        compiler_params=pltpu.CompilerParams(vmem_limit_bytes=24 * 1024 * 1024),
        cost_estimate=pl.CostEstimate(flops=1_000_000, bytes_accessed=10_000, transcendentals=0),
        name="own_projection",
    )(weights, gathered)


def mark_kernel(w_ref, out_ref):
    out_ref[...] = jnp.zeros_like(out_ref)


def arrival_mark(weights):
    return pl.pallas_call(
        mark_kernel,
        in_specs=[pl.BlockSpec(memory_space=pl.ANY)],
        out_shape=jax.ShapeDtypeStruct((8, 128), jnp.float32),
        cost_estimate=pl.CostEstimate(flops=MARK_FLOPS, bytes_accessed=1000, transcendentals=0),
        name="arrival_mark",
    )(weights)


def scaling_of(squares_ref, tail):
    tail = tail.astype(jnp.float32)
    total = jnp.sum(squares_ref[...], axis=0, keepdims=True) + tail[0:1] + tail[1:2]
    return lax.rsqrt(total * (1.0 / D) + epsilon)


def weigh_kernel(lengths_ref, own_ref, came_ref, squares_ref, expo_ref, rows_ref):
    scaling = scaling_of(squares_ref, came_ref[2 * HEAD :, :])
    both = (own_ref[: 2 * HEAD, :] + came_ref[: 2 * HEAD, :].astype(jnp.float32)) * scaling
    query = both[:HEAD, :].astype(jnp.bfloat16)
    keys = both[HEAD:, :].astype(jnp.bfloat16).T
    rows_ref[0:1, :] = scaling
    first = lengths_ref[0, 0]
    second = first + lengths_ref[0, 1]
    third = second + lengths_ref[0, 2]

    def scene(position):
        return (
            (position >= first).astype(jnp.int32)
            + (position >= second).astype(jnp.int32)
            + (position >= third).astype(jnp.int32)
        )

    key_scene = scene(lax.broadcasted_iota(jnp.int32, (TOK, 1), 0))
    for part in range(TOK // CHUNK):
        cols = slice(part * CHUNK, (part + 1) * CHUNK)
        query_scene = scene(lax.broadcasted_iota(jnp.int32, (1, CHUNK), 1) + part * CHUNK)
        scores = jnp.dot(keys, query[:, cols], preferred_element_type=jnp.float32)
        scores = jnp.where(key_scene == query_scene, scores * HEAD ** (-0.5), -jnp.inf)
        expo = jnp.exp(scores - jnp.max(scores, axis=0, keepdims=True))
        rows_ref[1:2, cols] = 1.0 / jnp.sum(expo, axis=0, keepdims=True)
        expo_ref[:, cols] = expo.astype(jnp.bfloat16)


def attention_weights(lengths, own, came, squares):
    whole = pl.BlockSpec(memory_space=pltpu.VMEM)
    return pl.pallas_call(
        weigh_kernel,
        in_specs=[pl.BlockSpec(memory_space=pltpu.SMEM)] + [whole] * 3,
        out_shape=(
            jax.ShapeDtypeStruct((TOK, TOK), jnp.bfloat16),
            jax.ShapeDtypeStruct((2, TOK), jnp.float32),
        ),
        compiler_params=pltpu.CompilerParams(vmem_limit_bytes=24 * 1024 * 1024),
        cost_estimate=pl.CostEstimate(flops=500_000_000, bytes_accessed=6_000_000, transcendentals=1_000_000),
        name="attention_weights",
    )(lengths, own, came, squares)


def mix_kernel(own_ref, came_ref, expo_ref, rows_ref, out_ref):
    values = (own_ref[2 * HEAD :, :] + came_ref[...].astype(jnp.float32)) * rows_ref[0:1, :]
    values = values.astype(jnp.bfloat16)
    for part in range(TOK // CHUNK):
        cols = slice(part * CHUNK, (part + 1) * CHUNK)
        mixed = jnp.dot(values, expo_ref[:, cols], preferred_element_type=jnp.float32)
        mixed = (mixed * rows_ref[1:2, cols]).astype(jnp.bfloat16)
        out_ref[:, cols] = mixed


def mix_values(own, came, expo, rows):
    return pl.pallas_call(
        mix_kernel,
        out_shape=jax.ShapeDtypeStruct((HEAD, TOK), jnp.bfloat16),
        compiler_params=pltpu.CompilerParams(vmem_limit_bytes=20 * 1024 * 1024),
        cost_estimate=pl.CostEstimate(flops=400_000_000, bytes_accessed=7_000_000, transcendentals=0),
        name="mix_values",
    )(own, came, expo, rows)


def copy_kernel(turn_ref, *refs):
    for in_ref, out_ref in zip(refs[:NX], refs[NX:]):
        out_ref[...] = in_ref[0]


def slice_columns(turn, weight):
    width = NZ * NY * HEAD

    def column_spec(k):
        return pl.BlockSpec((1, HEAD, width), lambda i, turn_ref: (0, 0, (turn_ref[0] + k) % NX))

    return pl.pallas_call(
        copy_kernel,
        grid_spec=pltpu.PrefetchScalarGridSpec(
            num_scalar_prefetch=1,
            grid=(1,),
            in_specs=[column_spec(k) for k in range(NX)],
            out_specs=[pl.BlockSpec((HEAD, width), lambda i, turn_ref: (0, 0))] * NX,
        ),
        out_shape=[jax.ShapeDtypeStruct((HEAD, width), jnp.bfloat16)] * NX,
        compiler_params=pltpu.CompilerParams(vmem_limit_bytes=48 * 1024 * 1024),
        cost_estimate=pl.CostEstimate(flops=0, bytes_accessed=5_000_000, transcendentals=0),
        name="slice_columns",
    )(turn, *[weight] * NX)


def project_kernel(w_ref, a0_ref, a1_ref, a2_ref, a3_ref, out_ref):
    heads = jnp.concatenate([ref[...] for ref in (a0_ref, a1_ref, a2_ref, a3_ref)], axis=0)
    out_ref[...] = jnp.dot(w_ref[...], heads, preferred_element_type=jnp.float32).astype(jnp.bfloat16)


def project(weight, heads):
    rows = NZ * NY * HEAD
    return pl.pallas_call(
        project_kernel,
        grid=(TOK // CHUNK,),
        in_specs=[pl.BlockSpec((rows, NX * HEAD), lambda k: (0, 0))]
        + [pl.BlockSpec((HEAD, CHUNK), lambda k: (0, k))] * NX,
        out_specs=pl.BlockSpec((rows, CHUNK), lambda k: (0, k)),
        out_shape=jax.ShapeDtypeStruct((rows, TOK), jnp.bfloat16),
        compiler_params=pltpu.CompilerParams(vmem_limit_bytes=24 * 1024 * 1024),
        cost_estimate=pl.CostEstimate(flops=2_500_000_000, bytes_accessed=7_000_000, transcendentals=0),
        name="project",
    )(weight, *heads)


def spread_kernel(parts_ref, received_ref, up_ref, middle_ref, out_ref):
    total = received_ref[...].astype(jnp.float32)
    head_sum = parts_ref[0].astype(jnp.float32)
    for x in range(1, NZ * NY):
        head_sum += parts_ref[x].astype(jnp.float32)
    middle = (total + head_sum).astype(jnp.bfloat16)
    middle_ref[...] = middle
    middle_f = middle.astype(jnp.float32)
    squares = jnp.sum(middle_f * middle_f, axis=0, keepdims=True)
    high = squares.astype(jnp.bfloat16).astype(jnp.float32)
    low = squares - high
    rows = [high[:, k * 128 : (k + 1) * 128] for k in range(8)] + [low[:, k * 128 : (k + 1) * 128] for k in range(8)]
    tile = jnp.concatenate(rows + [jnp.zeros((8, 128), jnp.float32)], axis=0)
    out_ref[:, TOK:] = jnp.concatenate([tile] * BLOCKS, axis=0).astype(jnp.bfloat16)
    out_ref[:, :TOK] = jnp.dot(up_ref[...], middle, preferred_element_type=jnp.float32).astype(jnp.bfloat16)


def spread_call(parts, received, up):
    return pl.pallas_call(
        spread_kernel,
        out_shape=(
            jax.ShapeDtypeStruct((HEAD, TOK), jnp.bfloat16),
            jax.ShapeDtypeStruct((WIDE, TOK + EXTRA), jnp.bfloat16),
        ),
        compiler_params=pltpu.CompilerParams(vmem_limit_bytes=20 * 1024 * 1024),
        cost_estimate=pl.CostEstimate(flops=310_000_000, bytes_accessed=5_000_000, transcendentals=0),
        name="spread",
    )(parts, received, up)


def hidden_kernel(up_ref, down_ref, r_ref, out_ref):
    sums = jnp.sum(r_ref[:, TOK:].astype(jnp.float32).reshape(BLOCKS, PIECE, 128), axis=0)
    sums = sums[0:8] + sums[8:16]
    total = jnp.concatenate([sums[k : k + 1] for k in range(8)], axis=1)
    scaling = lax.rsqrt(total * (1.0 / D) + epsilon)
    for part in range(TOK // CHUNK):
        cols = slice(part * CHUNK, (part + 1) * CHUNK)
        pre = jnp.dot(up_ref[...], r_ref[:, cols], preferred_element_type=jnp.float32) * scaling[:, cols]
        hidden = 0.5 * pre * (1.0 + jnp.tanh(0.7978845608028654 * (pre + 0.044715 * (pre * pre * pre))))
        out_ref[:, cols] = jnp.dot(
            down_ref[...], hidden.astype(jnp.bfloat16), preferred_element_type=jnp.float32
        ).astype(jnp.bfloat16)


def hidden_call(up, down, pieces):
    return pl.pallas_call(
        hidden_kernel,
        out_shape=jax.ShapeDtypeStruct((WIDE, TOK), jnp.bfloat16),
        compiler_params=pltpu.CompilerParams(vmem_limit_bytes=24 * 1024 * 1024),
        cost_estimate=pl.CostEstimate(flops=2_500_000_000, bytes_accessed=6_000_000, transcendentals=1_000_000),
        name="hidden",
    )(up, down, pieces)


def final_kernel(down_ref, b_ref, middle_ref, out_ref):
    out = jnp.dot(down_ref[...], b_ref[...], preferred_element_type=jnp.float32)
    out_ref[...] = (middle_ref[...].astype(jnp.float32) + out).astype(jnp.bfloat16)


def final_call(down, pieces, middle):
    return pl.pallas_call(
        final_kernel,
        out_shape=jax.ShapeDtypeStruct((HEAD, TOK), jnp.bfloat16),
        compiler_params=pltpu.CompilerParams(vmem_limit_bytes=16 * 1024 * 1024),
        cost_estimate=pl.CostEstimate(flops=310_000_000, bytes_accessed=3_000_000, transcendentals=0),
        name="final",
    )(down, pieces, middle)


TENSOR = ("x", "z", "y")


def shift_pairs(count):
    devices = NX * NZ * NY
    return [(t, (t + devices) % (count * devices)) for t in range(count * devices)]


SWAP = [(0, 1), (1, 0)]


def around_x(value, steps):
    return lax.ppermute(value, "x", [(x, (x + steps) % NX) for x in range(NX)])


def shards(
    incoming,
    scene_lengths,
    attn_gain,
    query_weight,
    key_weight,
    value_weight,
    output_weight,
    ffn_gain,
    up_first,
    up_second,
    down_first,
    down_second,
):
    everything = ("pipe",) + TENSOR
    count = lax.axis_size("pipe")
    received = lax.ppermute(incoming, everything, shift_pairs(count))
    place = lax.axis_index("z").astype(jnp.int32).reshape(1)
    weights = (attn_gain, query_weight, key_weight, value_weight)
    beside = half_weights(1 - place, *weights)
    ahead, _ = lax.optimization_barrier((received, beside))
    beside = lax.ppermute(beside, "z", SWAP)
    gathered = lax.all_gather(ahead, ("x", "y"), axis=0, tiled=True).reshape(NX, NY * HEAD, TOK)

    turn = lax.axis_index("x").astype(jnp.int32).reshape(1)
    tied = (ahead, *weights, output_weight, up_first, up_second, down_first, down_second, ffn_gain)
    tied = lax.optimization_barrier(tied)
    _, *weights, output_weight, up_first, up_second, down_first, down_second, ffn_gain = tied
    own_weights = half_weights(place, *weights)
    columns = slice_columns(turn, output_weight)
    up_first = (up_first.reshape(HEAD, WIDE).T.astype(jnp.float32) * ffn_gain).astype(jnp.bfloat16)
    up_second = up_second.reshape(WIDE, WIDE).T
    down_first = down_first.reshape(WIDE, WIDE).T
    down_second = down_second.reshape(WIDE, HEAD).T
    tied = (beside, own_weights, columns, up_first, up_second, down_first, down_second)
    tied = lax.optimization_barrier(tied)
    beside, own_weights, columns, up_first, up_second, down_first, down_second = tied
    mark = arrival_mark(beside)

    crossed, crossed_values, squares = cross_projection(beside, gathered, mark)
    came = lax.ppermute(crossed, "z", SWAP)
    came_values = lax.ppermute(crossed_values, "z", SWAP)
    _, gathered, columns = lax.optimization_barrier((crossed, gathered, columns))
    own = own_projection(own_weights, gathered)
    blocks = [columns[0]] + [around_x(columns[k], k) for k in range(1, NX)]
    out_weight = jnp.concatenate(blocks, axis=0).T

    expo, rows = attention_weights(scene_lengths, own, came, squares)
    attended = mix_values(own, came_values, expo, rows)
    heads = [attended] + [around_x(attended, k) for k in range(1, NX)]
    partial = project(out_weight, heads)
    parts = lax.all_to_all(
        partial.reshape(NZ * NY, HEAD, TOK), ("z", "y"), split_axis=0, concat_axis=0, tiled=True
    )
    middle, spread = spread_call(parts, received, up_first)
    pieces = lax.all_to_all(
        spread.reshape(BLOCKS, PIECE, TOK + EXTRA), TENSOR, split_axis=0, concat_axis=0, tiled=True
    )
    mixed_back = hidden_call(up_second, down_first, pieces.reshape(WIDE, TOK + EXTRA))
    returned = lax.all_to_all(
        mixed_back.reshape(BLOCKS, PIECE, TOK), TENSOR, split_axis=0, concat_axis=0, tiled=True
    )
    return final_call(down_second, returned.reshape(WIDE, TOK), middle)


def solution(mesh):
    devices = mesh.devices
    finer = Mesh(devices.reshape(devices.shape[0], NX, NZ, NY), ("pipe",) + TENSOR)
    return jax.shard_map(
        shards,
        mesh=finer,
        in_specs=(
            P(TENSOR, "pipe"),
            P("pipe", None),
            P("pipe", None),
            P("pipe", TENSOR, None),
            P("pipe", TENSOR, None),
            P("pipe", TENSOR, None),
            P("pipe", TENSOR, None),
            P("pipe", TENSOR),
            P("pipe", TENSOR, None, None),
            P("pipe", TENSOR, None, None),
            P("pipe", TENSOR, None, None),
            P("pipe", TENSOR, None, None),
        ),
        out_specs=P(TENSOR, "pipe"),
        check_vma=False,
    )
```

```python
import functools

import jax
import jax.numpy as jnp
from jax import lax
from jax.experimental import pallas as pl
from jax.experimental.pallas import tpu as pltpu
from jax.sharding import Mesh, PartitionSpec as P

D = 6144
HEAD = 192
TOK = 1024
BLOCKS = 32
PIECE = 24
WIDE = 768
CHUNK = 256
NX, NZ, NY = 4, 2, 4
PART = NX // 2
EXTRA = 128
MARK_FLOPS = 110_000_000_000

epsilon = 1e-06


def scale_kernel(half_ref, gain_ref, wq_ref, wk_ref, wv_ref, out_ref):
    gain = gain_ref[...]
    for part, ref in enumerate((wq_ref, wk_ref, wv_ref)):
        out_ref[0, part * HEAD : (part + 1) * HEAD, :] = (ref[0].astype(jnp.float32) * gain).astype(jnp.bfloat16)


def half_weights(first, count, half, gain, query_weight, key_weight, value_weight):
    weight_spec = pl.BlockSpec((1, HEAD, WIDE), lambda k, half_ref: (0, 0, 2 * (k + first) + half_ref[0]))
    return pl.pallas_call(
        scale_kernel,
        grid_spec=pltpu.PrefetchScalarGridSpec(
            num_scalar_prefetch=1,
            grid=(count,),
            in_specs=[
                pl.BlockSpec((1, WIDE), lambda k, half_ref: (0, 2 * (k + first) + half_ref[0])),
                weight_spec,
                weight_spec,
                weight_spec,
            ],
            out_specs=pl.BlockSpec((1, 3 * HEAD, WIDE), lambda k, half_ref: (k, 0, 0)),
        ),
        out_shape=jax.ShapeDtypeStruct((count, 3 * HEAD, WIDE), jnp.bfloat16),
        compiler_params=pltpu.CompilerParams(vmem_limit_bytes=58 * 1024 * 1024),
        cost_estimate=pl.CostEstimate(flops=0, bytes_accessed=7_000_000, transcendentals=0),
        name="half_weights",
    )(half, gain, query_weight, key_weight, value_weight)


def accumulate(product, acc_ref):
    @pl.when(pl.program_id(0) == 0)
    def _():
        acc_ref[...] = product

    @pl.when(pl.program_id(0) > 0)
    def _():
        acc_ref[...] += product


def cross_kernel(
    w0_ref, w1_ref, g_ref, mark_ref, out_ref, values_ref, squares_ref, w_buffer, g_buffer, acc_ref, w_sems, g_sems
):
    for k in range(NX):
        source = w0_ref.at[k] if k < PART else w1_ref.at[k - PART]
        pltpu.make_async_copy(source, w_buffer.at[k], w_sems.at[k]).start()
        pltpu.make_async_copy(g_ref.at[k], g_buffer.at[k], g_sems.at[k]).start()
    for k in range(NX):
        source = w0_ref.at[k] if k < PART else w1_ref.at[k - PART]
        pltpu.make_async_copy(source, w_buffer.at[k], w_sems.at[k]).wait()
        pltpu.make_async_copy(g_ref.at[k], g_buffer.at[k], g_sems.at[k]).wait()
        block = g_buffer[k]
        block_f = block.astype(jnp.float32)
        squares = jnp.sum((block_f * block_f).reshape(WIDE // 8, 8, TOK), axis=0)
        squares_ref[...] = squares if k == 0 else squares_ref[...] + squares
        for part in range(2):
            cols = slice(part * (TOK // 2), (part + 1) * (TOK // 2))
            product = jnp.dot(w_buffer[k], block[:, cols], preferred_element_type=jnp.float32)
            if k > 0:
                product = acc_ref[:, cols] + product
            if k < NX - 1:
                acc_ref[:, cols] = product
            else:
                out_ref[: 2 * HEAD, cols] = product[: 2 * HEAD].astype(jnp.bfloat16)
                values_ref[:, cols] = product[2 * HEAD :].astype(jnp.bfloat16)
    total = jnp.sum(squares_ref[...], axis=0, keepdims=True)
    high = total.astype(jnp.bfloat16).astype(jnp.float32)
    tail = jnp.concatenate([high, total - high, jnp.zeros((14, TOK), jnp.float32)], axis=0)
    out_ref[2 * HEAD :, :] = tail.astype(jnp.bfloat16)


def cross_projection(first, second, gathered, mark):
    return pl.pallas_call(
        cross_kernel,
        in_specs=[pl.BlockSpec(memory_space=pl.ANY)] * 4,
        out_shape=(
            jax.ShapeDtypeStruct((2 * HEAD + 16, TOK), jnp.bfloat16),
            jax.ShapeDtypeStruct((HEAD, TOK), jnp.bfloat16),
            jax.ShapeDtypeStruct((8, TOK), jnp.float32),
        ),
        scratch_shapes=[
            pltpu.VMEM((NX, 3 * HEAD, WIDE), jnp.bfloat16),
            pltpu.VMEM((NX, WIDE, TOK), jnp.bfloat16),
            pltpu.VMEM((3 * HEAD, TOK), jnp.float32),
            pltpu.SemaphoreType.DMA((NX,)),
            pltpu.SemaphoreType.DMA((NX,)),
        ],
        compiler_params=pltpu.CompilerParams(vmem_limit_bytes=58 * 1024 * 1024),
        cost_estimate=pl.CostEstimate(flops=1_000_000, bytes_accessed=10_000, transcendentals=0),
        name="cross_projection",
    )(first, second, gathered, mark)


def own_kernel(w_ref, g_ref, out_ref):
    accumulate(jnp.dot(w_ref[0], g_ref[0], preferred_element_type=jnp.float32), out_ref)


def own_projection(weights, gathered):
    return pl.pallas_call(
        own_kernel,
        grid=(NX,),
        in_specs=[
            pl.BlockSpec((1, 3 * HEAD, WIDE), lambda k: (k, 0, 0)),
            pl.BlockSpec((1, WIDE, TOK), lambda k: (k, 0, 0)),
        ],
        out_specs=pl.BlockSpec((3 * HEAD, TOK), lambda k: (0, 0)),
        out_shape=jax.ShapeDtypeStruct((3 * HEAD, TOK), jnp.float32),
        compiler_params=pltpu.CompilerParams(vmem_limit_bytes=24 * 1024 * 1024),
        cost_estimate=pl.CostEstimate(flops=1_000_000, bytes_accessed=10_000, transcendentals=0),
        name="own_projection",
    )(weights, gathered)


def mark_kernel(w_ref, out_ref):
    out_ref[...] = jnp.zeros_like(out_ref)


def arrival_mark(weights):
    return pl.pallas_call(
        mark_kernel,
        in_specs=[pl.BlockSpec(memory_space=pl.ANY)],
        out_shape=jax.ShapeDtypeStruct((8, 128), jnp.float32),
        cost_estimate=pl.CostEstimate(flops=MARK_FLOPS, bytes_accessed=1000, transcendentals=0),
        name="arrival_mark",
    )(weights)


def scaling_of(squares_ref, tail):
    tail = tail.astype(jnp.float32)
    total = jnp.sum(squares_ref[...], axis=0, keepdims=True) + tail[0:1] + tail[1:2]
    return lax.rsqrt(total * (1.0 / D) + epsilon)


def weigh_kernel(lengths_ref, own_ref, came_ref, squares_ref, expo_ref, rows_ref):
    scaling = scaling_of(squares_ref, came_ref[2 * HEAD :, :])
    both = (own_ref[: 2 * HEAD, :] + came_ref[: 2 * HEAD, :].astype(jnp.float32)) * scaling
    query = both[:HEAD, :].astype(jnp.bfloat16)
    keys = both[HEAD:, :].astype(jnp.bfloat16).T
    rows_ref[0:1, :] = scaling
    first = lengths_ref[0, 0]
    second = first + lengths_ref[0, 1]
    third = second + lengths_ref[0, 2]

    def scene(position):
        return (
            (position >= first).astype(jnp.int32)
            + (position >= second).astype(jnp.int32)
            + (position >= third).astype(jnp.int32)
        )

    key_scene = scene(lax.broadcasted_iota(jnp.int32, (TOK, 1), 0))
    for part in range(TOK // CHUNK):
        cols = slice(part * CHUNK, (part + 1) * CHUNK)
        query_scene = scene(lax.broadcasted_iota(jnp.int32, (1, CHUNK), 1) + part * CHUNK)
        scores = jnp.dot(keys, query[:, cols], preferred_element_type=jnp.float32)
        scores = jnp.where(key_scene == query_scene, scores * HEAD ** (-0.5), -jnp.inf)
        expo = jnp.exp(scores - jnp.max(scores, axis=0, keepdims=True))
        rows_ref[1:2, cols] = 1.0 / jnp.sum(expo, axis=0, keepdims=True)
        expo_ref[:, cols] = expo.astype(jnp.bfloat16)


def attention_weights(lengths, own, came, squares):
    whole = pl.BlockSpec(memory_space=pltpu.VMEM)
    return pl.pallas_call(
        weigh_kernel,
        in_specs=[pl.BlockSpec(memory_space=pltpu.SMEM)] + [whole] * 3,
        out_shape=(
            jax.ShapeDtypeStruct((TOK, TOK), jnp.bfloat16),
            jax.ShapeDtypeStruct((2, TOK), jnp.float32),
        ),
        compiler_params=pltpu.CompilerParams(vmem_limit_bytes=24 * 1024 * 1024),
        cost_estimate=pl.CostEstimate(flops=500_000_000, bytes_accessed=6_000_000, transcendentals=1_000_000),
        name="attention_weights",
    )(lengths, own, came, squares)


def mix_kernel(own_ref, came_ref, expo_ref, rows_ref, out_ref):
    values = (own_ref[2 * HEAD :, :] + came_ref[...].astype(jnp.float32)) * rows_ref[0:1, :]
    values = values.astype(jnp.bfloat16)
    for part in range(TOK // CHUNK):
        cols = slice(part * CHUNK, (part + 1) * CHUNK)
        mixed = jnp.dot(values, expo_ref[:, cols], preferred_element_type=jnp.float32)
        mixed = (mixed * rows_ref[1:2, cols]).astype(jnp.bfloat16)
        out_ref[:, cols] = mixed


def mix_values(own, came, expo, rows):
    return pl.pallas_call(
        mix_kernel,
        out_shape=jax.ShapeDtypeStruct((HEAD, TOK), jnp.bfloat16),
        compiler_params=pltpu.CompilerParams(vmem_limit_bytes=20 * 1024 * 1024),
        cost_estimate=pl.CostEstimate(flops=400_000_000, bytes_accessed=7_000_000, transcendentals=0),
        name="mix_values",
    )(own, came, expo, rows)


def copy_kernel(turn_ref, *refs):
    for in_ref, out_ref in zip(refs[:NX], refs[NX:]):
        out_ref[...] = in_ref[0]


def slice_columns(turn, weight):
    width = NZ * NY * HEAD

    def column_spec(k):
        return pl.BlockSpec((1, HEAD, width), lambda i, turn_ref: (0, 0, (turn_ref[0] + k) % NX))

    return pl.pallas_call(
        copy_kernel,
        grid_spec=pltpu.PrefetchScalarGridSpec(
            num_scalar_prefetch=1,
            grid=(1,),
            in_specs=[column_spec(k) for k in range(NX)],
            out_specs=[pl.BlockSpec((HEAD, width), lambda i, turn_ref: (0, 0))] * NX,
        ),
        out_shape=[jax.ShapeDtypeStruct((HEAD, width), jnp.bfloat16)] * NX,
        compiler_params=pltpu.CompilerParams(vmem_limit_bytes=48 * 1024 * 1024),
        cost_estimate=pl.CostEstimate(flops=0, bytes_accessed=5_000_000, transcendentals=0),
        name="slice_columns",
    )(turn, *[weight] * NX)


def project_kernel(w_ref, a0_ref, a1_ref, a2_ref, a3_ref, out_ref):
    heads = jnp.concatenate([ref[...] for ref in (a0_ref, a1_ref, a2_ref, a3_ref)], axis=0)
    out_ref[...] = jnp.dot(w_ref[...], heads, preferred_element_type=jnp.float32).astype(jnp.bfloat16)


def project(weight, heads):
    rows = NZ * NY * HEAD
    return pl.pallas_call(
        project_kernel,
        grid=(TOK // CHUNK,),
        in_specs=[pl.BlockSpec((rows, NX * HEAD), lambda k: (0, 0))]
        + [pl.BlockSpec((HEAD, CHUNK), lambda k: (0, k))] * NX,
        out_specs=pl.BlockSpec((rows, CHUNK), lambda k: (0, k)),
        out_shape=jax.ShapeDtypeStruct((rows, TOK), jnp.bfloat16),
        compiler_params=pltpu.CompilerParams(vmem_limit_bytes=24 * 1024 * 1024),
        cost_estimate=pl.CostEstimate(flops=2_500_000_000, bytes_accessed=7_000_000, transcendentals=0),
        name="project",
    )(weight, *heads)


def spread_kernel(parts_ref, received_ref, up_ref, middle_ref, out_ref):
    total = received_ref[...].astype(jnp.float32)
    head_sum = parts_ref[0].astype(jnp.float32)
    for x in range(1, NZ * NY):
        head_sum += parts_ref[x].astype(jnp.float32)
    middle = (total + head_sum).astype(jnp.bfloat16)
    middle_ref[...] = middle
    middle_f = middle.astype(jnp.float32)
    squares = jnp.sum(middle_f * middle_f, axis=0, keepdims=True)
    high = squares.astype(jnp.bfloat16).astype(jnp.float32)
    low = squares - high
    rows = [high[:, k * 128 : (k + 1) * 128] for k in range(8)] + [low[:, k * 128 : (k + 1) * 128] for k in range(8)]
    tile = jnp.concatenate(rows + [jnp.zeros((8, 128), jnp.float32)], axis=0)
    out_ref[:, TOK:] = jnp.concatenate([tile] * BLOCKS, axis=0).astype(jnp.bfloat16)
    out_ref[:, :TOK] = jnp.dot(up_ref[...], middle, preferred_element_type=jnp.float32).astype(jnp.bfloat16)


def spread_call(parts, received, up):
    return pl.pallas_call(
        spread_kernel,
        out_shape=(
            jax.ShapeDtypeStruct((HEAD, TOK), jnp.bfloat16),
            jax.ShapeDtypeStruct((WIDE, TOK + EXTRA), jnp.bfloat16),
        ),
        compiler_params=pltpu.CompilerParams(vmem_limit_bytes=20 * 1024 * 1024),
        cost_estimate=pl.CostEstimate(flops=310_000_000, bytes_accessed=5_000_000, transcendentals=0),
        name="spread",
    )(parts, received, up)


def hidden_kernel(up_ref, down_ref, r_ref, out_ref):
    sums = jnp.sum(r_ref[:, TOK:].astype(jnp.float32).reshape(BLOCKS, PIECE, 128), axis=0)
    sums = sums[0:8] + sums[8:16]
    total = jnp.concatenate([sums[k : k + 1] for k in range(8)], axis=1)
    scaling = lax.rsqrt(total * (1.0 / D) + epsilon)
    for part in range(TOK // CHUNK):
        cols = slice(part * CHUNK, (part + 1) * CHUNK)
        pre = jnp.dot(up_ref[...], r_ref[:, cols], preferred_element_type=jnp.float32) * scaling[:, cols]
        hidden = 0.5 * pre * (1.0 + jnp.tanh(0.7978845608028654 * (pre + 0.044715 * (pre * pre * pre))))
        out_ref[:, cols] = jnp.dot(
            down_ref[...], hidden.astype(jnp.bfloat16), preferred_element_type=jnp.float32
        ).astype(jnp.bfloat16)


def hidden_call(up, down, pieces):
    return pl.pallas_call(
        hidden_kernel,
        out_shape=jax.ShapeDtypeStruct((WIDE, TOK), jnp.bfloat16),
        compiler_params=pltpu.CompilerParams(vmem_limit_bytes=24 * 1024 * 1024),
        cost_estimate=pl.CostEstimate(flops=2_500_000_000, bytes_accessed=6_000_000, transcendentals=1_000_000),
        name="hidden",
    )(up, down, pieces)


def final_kernel(down_ref, b_ref, middle_ref, out_ref):
    out = jnp.dot(down_ref[...], b_ref[...], preferred_element_type=jnp.float32)
    out_ref[...] = (middle_ref[...].astype(jnp.float32) + out).astype(jnp.bfloat16)


def final_call(down, pieces, middle):
    return pl.pallas_call(
        final_kernel,
        out_shape=jax.ShapeDtypeStruct((HEAD, TOK), jnp.bfloat16),
        compiler_params=pltpu.CompilerParams(vmem_limit_bytes=16 * 1024 * 1024),
        cost_estimate=pl.CostEstimate(flops=310_000_000, bytes_accessed=3_000_000, transcendentals=0),
        name="final",
    )(down, pieces, middle)


TENSOR = ("x", "z", "y")


def shift_pairs(count):
    devices = NX * NZ * NY
    return [(t, (t + devices) % (count * devices)) for t in range(count * devices)]


SWAP = [(0, 1), (1, 0)]


def around_x(value, steps):
    return lax.ppermute(value, "x", [(x, (x + steps) % NX) for x in range(NX)])


def shards(
    incoming,
    scene_lengths,
    attn_gain,
    query_weight,
    key_weight,
    value_weight,
    output_weight,
    ffn_gain,
    up_first,
    up_second,
    down_first,
    down_second,
):
    everything = ("pipe",) + TENSOR
    count = lax.axis_size("pipe")
    received = lax.ppermute(incoming, everything, shift_pairs(count))
    place = lax.axis_index("z").astype(jnp.int32).reshape(1)
    weights = (attn_gain, query_weight, key_weight, value_weight)
    first = half_weights(0, PART, 1 - place, *weights)
    second = half_weights(PART, NX - PART, 1 - place, *weights)
    ahead, _ = lax.optimization_barrier((received, first))
    first = lax.ppermute(first, "z", SWAP)
    second = lax.ppermute(second, "z", SWAP)
    gathered = lax.all_gather(ahead, ("x", "y"), axis=0, tiled=True).reshape(NX, NY * HEAD, TOK)

    turn = lax.axis_index("x").astype(jnp.int32).reshape(1)
    tied = (ahead, *weights, output_weight, up_first, up_second, down_first, down_second, ffn_gain)
    tied = lax.optimization_barrier(tied)
    _, *weights, output_weight, up_first, up_second, down_first, down_second, ffn_gain = tied
    own_weights = half_weights(0, NX, place, *weights)
    columns = slice_columns(turn, output_weight)
    up_first = (up_first.reshape(HEAD, WIDE).T.astype(jnp.float32) * ffn_gain).astype(jnp.bfloat16)
    up_second = up_second.reshape(WIDE, WIDE).T
    down_first = down_first.reshape(WIDE, WIDE).T
    down_second = down_second.reshape(WIDE, HEAD).T
    tied = (first, own_weights, columns, up_first, up_second, down_first, down_second)
    tied = lax.optimization_barrier(tied)
    first, own_weights, columns, up_first, up_second, down_first, down_second = tied
    mark = arrival_mark(first)

    crossed, crossed_values, squares = cross_projection(first, second, gathered, mark)
    came = lax.ppermute(crossed, "z", SWAP)
    came_values = lax.ppermute(crossed_values, "z", SWAP)
    _, gathered, columns = lax.optimization_barrier((crossed, gathered, columns))
    own = own_projection(own_weights, gathered)
    blocks = [columns[0]] + [around_x(columns[k], k) for k in range(1, NX)]
    out_weight = jnp.concatenate(blocks, axis=0).T

    expo, rows = attention_weights(scene_lengths, own, came, squares)
    attended = mix_values(own, came_values, expo, rows)
    heads = [attended] + [around_x(attended, k) for k in range(1, NX)]
    partial = project(out_weight, heads)
    parts = lax.all_to_all(
        partial.reshape(NZ * NY, HEAD, TOK), ("z", "y"), split_axis=0, concat_axis=0, tiled=True
    )
    middle, spread = spread_call(parts, received, up_first)
    pieces = lax.all_to_all(
        spread.reshape(BLOCKS, PIECE, TOK + EXTRA), TENSOR, split_axis=0, concat_axis=0, tiled=True
    )
    mixed_back = hidden_call(up_second, down_first, pieces.reshape(WIDE, TOK + EXTRA))
    returned = lax.all_to_all(
        mixed_back.reshape(BLOCKS, PIECE, TOK), TENSOR, split_axis=0, concat_axis=0, tiled=True
    )
    return final_call(down_second, returned.reshape(WIDE, TOK), middle)


def solution(mesh):
    devices = mesh.devices
    finer = Mesh(devices.reshape(devices.shape[0], NX, NZ, NY), ("pipe",) + TENSOR)
    return jax.shard_map(
        shards,
        mesh=finer,
        in_specs=(
            P(TENSOR, "pipe"),
            P("pipe", None),
            P("pipe", None),
            P("pipe", TENSOR, None),
            P("pipe", TENSOR, None),
            P("pipe", TENSOR, None),
            P("pipe", TENSOR, None),
            P("pipe", TENSOR),
            P("pipe", TENSOR, None, None),
            P("pipe", TENSOR, None, None),
            P("pipe", TENSOR, None, None),
            P("pipe", TENSOR, None, None),
        ),
        out_specs=P(TENSOR, "pipe"),
        check_vma=False,
    )
```

```python
import functools

import jax
import jax.numpy as jnp
from jax import lax
from jax.experimental import pallas as pl
from jax.experimental.pallas import tpu as pltpu
from jax.sharding import Mesh, PartitionSpec as P

D = 6144
HEAD = 192
TOK = 1024
BLOCKS = 32
PIECE = 24
WIDE = 768
CHUNK = 256
NX, NZ, NY = 4, 2, 4
PART = NX // 2
EXTRA = 128
HALF = TOK // 2
CROSS_LIMIT = 40
MARK_FLOPS = 1_000_000

epsilon = 1e-06


def scale_kernel(half_ref, gain_ref, wq_ref, wk_ref, wv_ref, out_ref):
    gain = gain_ref[...]
    for part, ref in enumerate((wq_ref, wk_ref, wv_ref)):
        out_ref[0, part * HEAD : (part + 1) * HEAD, :] = (ref[0].astype(jnp.float32) * gain).astype(jnp.bfloat16)


def half_weights(first, count, half, gain, query_weight, key_weight, value_weight):
    weight_spec = pl.BlockSpec((1, HEAD, WIDE), lambda k, half_ref: (0, 0, 2 * (k + first) + half_ref[0]))
    return pl.pallas_call(
        scale_kernel,
        grid_spec=pltpu.PrefetchScalarGridSpec(
            num_scalar_prefetch=1,
            grid=(count,),
            in_specs=[
                pl.BlockSpec((1, WIDE), lambda k, half_ref: (0, 2 * (k + first) + half_ref[0])),
                weight_spec,
                weight_spec,
                weight_spec,
            ],
            out_specs=pl.BlockSpec((1, 3 * HEAD, WIDE), lambda k, half_ref: (k, 0, 0)),
        ),
        out_shape=jax.ShapeDtypeStruct((count, 3 * HEAD, WIDE), jnp.bfloat16),
        compiler_params=pltpu.CompilerParams(vmem_limit_bytes=58 * 1024 * 1024),
        cost_estimate=pl.CostEstimate(flops=0, bytes_accessed=7_000_000, transcendentals=0),
        name="half_weights",
    )(half, gain, query_weight, key_weight, value_weight)


def accumulate(product, acc_ref):
    @pl.when(pl.program_id(0) == 0)
    def _():
        acc_ref[...] = product

    @pl.when(pl.program_id(0) > 0)
    def _():
        acc_ref[...] += product


def block_copies(x, place_ref, wide_refs, tall_ref, g_buffer, sems):
    copies = []
    for j in range(NY):
        rows = pl.ds(pl.multiple_of(lax.rem(place_ref[0] + NY - j, NY) * HEAD, HEAD), HEAD)
        copies.append(pltpu.make_async_copy(wide_refs[j].at[x], g_buffer.at[x, rows, pl.ds(0, HALF)], sems.at[x, j]))
        copies.append(
            pltpu.make_async_copy(tall_ref.at[x, j], g_buffer.at[x, rows, pl.ds(HALF, HALF)], sems.at[x, NY + j])
        )
    return x, copies


def cross_kernel(place_ref, w_ref, *refs):
    wide_refs, tall_ref = refs[:NY], refs[NY]
    out_ref, values_ref, squares_ref, w_buffer, g_buffer, acc_ref, w_sems, g_sems = refs[NY + 2 :]
    weights = [pltpu.make_async_copy(w_ref.at[k], w_buffer.at[k], w_sems.at[k]) for k in range(NX)]
    for copy in weights:
        copy.start()
    steps = [block_copies(step, place_ref, wide_refs, tall_ref, g_buffer, g_sems) for step in range(NX)]
    for _, copies in steps:
        for copy in copies:
            copy.start()
    for copy in weights:
        copy.wait()
    for step, (x, copies) in enumerate(steps):
        for copy in copies:
            copy.wait()
        block = g_buffer[x]
        weight = w_buffer[x]
        block_f = block.astype(jnp.float32)
        squares = jnp.sum((block_f * block_f).reshape(WIDE // 8, 8, TOK), axis=0)
        squares_ref[...] = squares if step == 0 else squares_ref[...] + squares
        for part in range(2):
            cols = slice(part * HALF, (part + 1) * HALF)
            product = jnp.dot(weight, block[:, cols], preferred_element_type=jnp.float32)
            if step > 0:
                product = acc_ref[:, cols] + product
            if step < NX - 1:
                acc_ref[:, cols] = product
            else:
                out_ref[: 2 * HEAD, cols] = product[: 2 * HEAD].astype(jnp.bfloat16)
                values_ref[:, cols] = product[2 * HEAD :].astype(jnp.bfloat16)
    total = jnp.sum(squares_ref[...], axis=0, keepdims=True)
    high = total.astype(jnp.bfloat16).astype(jnp.float32)
    tail = jnp.concatenate([high, total - high, jnp.zeros((14, TOK), jnp.float32)], axis=0)
    out_ref[2 * HEAD :, :] = tail.astype(jnp.bfloat16)


def cross_projection(place, weights, wide, tall, mark):
    return pl.pallas_call(
        cross_kernel,
        in_specs=[pl.BlockSpec(memory_space=pltpu.SMEM)] + [pl.BlockSpec(memory_space=pl.ANY)] * (3 + NY),
        out_shape=(
            jax.ShapeDtypeStruct((2 * HEAD + 16, TOK), jnp.bfloat16),
            jax.ShapeDtypeStruct((HEAD, TOK), jnp.bfloat16),
            jax.ShapeDtypeStruct((8, TOK), jnp.float32),
        ),
        scratch_shapes=[
            pltpu.VMEM((NX, 3 * HEAD, WIDE), jnp.bfloat16),
            pltpu.VMEM((NX, WIDE, TOK), jnp.bfloat16),
            pltpu.VMEM((3 * HEAD, TOK), jnp.float32),
            pltpu.SemaphoreType.DMA((NX,)),
            pltpu.SemaphoreType.DMA((NX, 2 * NY)),
        ],
        compiler_params=pltpu.CompilerParams(vmem_limit_bytes=CROSS_LIMIT * 1024 * 1024),
        cost_estimate=pl.CostEstimate(flops=1_000_000, bytes_accessed=10_000, transcendentals=0),
        name="cross_projection",
    )(place, weights, *wide, tall, mark)


def own_kernel(place_ref, w_ref, *refs):
    wide_refs, tall_ref = refs[:NY], refs[NY]
    out_ref, w_buffer, g_buffer, w_sem, g_sems = refs[NY + 1 :]
    weights = pltpu.make_async_copy(w_ref, w_buffer, w_sem)
    weights.start()
    steps = [block_copies(step, place_ref, wide_refs, tall_ref, g_buffer, g_sems) for step in range(NX)]
    for _, copies in steps:
        for copy in copies:
            copy.start()
    weights.wait()
    for step, (x, copies) in enumerate(steps):
        for copy in copies:
            copy.wait()
        for part in range(2):
            cols = slice(part * HALF, (part + 1) * HALF)
            product = jnp.dot(w_buffer[x], g_buffer[x, :, cols], preferred_element_type=jnp.float32)
            out_ref[:, cols] = product if step == 0 else out_ref[:, cols] + product


def own_projection(place, weights, wide, tall):
    return pl.pallas_call(
        own_kernel,
        in_specs=[pl.BlockSpec(memory_space=pltpu.SMEM)] + [pl.BlockSpec(memory_space=pl.ANY)] * (2 + NY),
        out_shape=jax.ShapeDtypeStruct((3 * HEAD, TOK), jnp.float32),
        scratch_shapes=[
            pltpu.VMEM((NX, 3 * HEAD, WIDE), jnp.bfloat16),
            pltpu.VMEM((NX, WIDE, TOK), jnp.bfloat16),
            pltpu.SemaphoreType.DMA,
            pltpu.SemaphoreType.DMA((NX, 2 * NY)),
        ],
        compiler_params=pltpu.CompilerParams(vmem_limit_bytes=32 * 1024 * 1024),
        cost_estimate=pl.CostEstimate(flops=1_000_000, bytes_accessed=10_000, transcendentals=0),
        name="own_projection",
    )(place, weights, *wide, tall)


def mark_kernel(w_ref, out_ref):
    out_ref[...] = jnp.zeros_like(out_ref)


def arrival_mark(weights):
    return pl.pallas_call(
        mark_kernel,
        in_specs=[pl.BlockSpec(memory_space=pl.ANY)],
        out_shape=jax.ShapeDtypeStruct((8, 128), jnp.float32),
        cost_estimate=pl.CostEstimate(flops=MARK_FLOPS, bytes_accessed=1000, transcendentals=0),
        name="arrival_mark",
    )(weights)


def scaling_of(squares_ref, tail):
    tail = tail.astype(jnp.float32)
    total = jnp.sum(squares_ref[...], axis=0, keepdims=True) + tail[0:1] + tail[1:2]
    return lax.rsqrt(total * (1.0 / D) + epsilon)


def weigh_kernel(lengths_ref, own_ref, came_ref, squares_ref, expo_ref, rows_ref):
    scaling = scaling_of(squares_ref, came_ref[2 * HEAD :, :])
    both = (own_ref[: 2 * HEAD, :] + came_ref[: 2 * HEAD, :].astype(jnp.float32)) * scaling
    query = both[:HEAD, :].astype(jnp.bfloat16)
    keys = both[HEAD:, :].astype(jnp.bfloat16).T
    rows_ref[0:1, :] = scaling
    first = lengths_ref[0, 0]
    second = first + lengths_ref[0, 1]
    third = second + lengths_ref[0, 2]

    def scene(position):
        return (
            (position >= first).astype(jnp.int32)
            + (position >= second).astype(jnp.int32)
            + (position >= third).astype(jnp.int32)
        )

    key_scene = scene(lax.broadcasted_iota(jnp.int32, (TOK, 1), 0))
    for part in range(TOK // CHUNK):
        cols = slice(part * CHUNK, (part + 1) * CHUNK)
        query_scene = scene(lax.broadcasted_iota(jnp.int32, (1, CHUNK), 1) + part * CHUNK)
        scores = jnp.dot(keys, query[:, cols], preferred_element_type=jnp.float32)
        scores = jnp.where(key_scene == query_scene, scores * HEAD ** (-0.5), -jnp.inf)
        expo = jnp.exp(scores - jnp.max(scores, axis=0, keepdims=True))
        rows_ref[1:2, cols] = 1.0 / jnp.sum(expo, axis=0, keepdims=True)
        expo_ref[:, cols] = expo.astype(jnp.bfloat16)


def attention_weights(lengths, own, came, squares):
    whole = pl.BlockSpec(memory_space=pltpu.VMEM)
    return pl.pallas_call(
        weigh_kernel,
        in_specs=[pl.BlockSpec(memory_space=pltpu.SMEM)] + [whole] * 3,
        out_shape=(
            jax.ShapeDtypeStruct((TOK, TOK), jnp.bfloat16),
            jax.ShapeDtypeStruct((2, TOK), jnp.float32),
        ),
        compiler_params=pltpu.CompilerParams(vmem_limit_bytes=24 * 1024 * 1024),
        cost_estimate=pl.CostEstimate(flops=500_000_000, bytes_accessed=6_000_000, transcendentals=1_000_000),
        name="attention_weights",
    )(lengths, own, came, squares)


def mix_kernel(own_ref, came_ref, expo_ref, rows_ref, out_ref):
    values = (own_ref[2 * HEAD :, :] + came_ref[...].astype(jnp.float32)) * rows_ref[0:1, :]
    values = values.astype(jnp.bfloat16)
    for part in range(TOK // CHUNK):
        cols = slice(part * CHUNK, (part + 1) * CHUNK)
        mixed = jnp.dot(values, expo_ref[:, cols], preferred_element_type=jnp.float32)
        mixed = (mixed * rows_ref[1:2, cols]).astype(jnp.bfloat16)
        out_ref[:, cols] = mixed


def mix_values(own, came, expo, rows):
    return pl.pallas_call(
        mix_kernel,
        out_shape=jax.ShapeDtypeStruct((HEAD, TOK), jnp.bfloat16),
        compiler_params=pltpu.CompilerParams(vmem_limit_bytes=20 * 1024 * 1024),
        cost_estimate=pl.CostEstimate(flops=400_000_000, bytes_accessed=7_000_000, transcendentals=0),
        name="mix_values",
    )(own, came, expo, rows)


def copy_kernel(turn_ref, *refs):
    for in_ref, out_ref in zip(refs[:NX], refs[NX:]):
        out_ref[...] = in_ref[0]


def slice_columns(turn, weight):
    width = NZ * NY * HEAD

    def column_spec(k):
        return pl.BlockSpec((1, HEAD, width), lambda i, turn_ref: (0, 0, (turn_ref[0] + k) % NX))

    return pl.pallas_call(
        copy_kernel,
        grid_spec=pltpu.PrefetchScalarGridSpec(
            num_scalar_prefetch=1,
            grid=(1,),
            in_specs=[column_spec(k) for k in range(NX)],
            out_specs=[pl.BlockSpec((HEAD, width), lambda i, turn_ref: (0, 0))] * NX,
        ),
        out_shape=[jax.ShapeDtypeStruct((HEAD, width), jnp.bfloat16)] * NX,
        compiler_params=pltpu.CompilerParams(vmem_limit_bytes=48 * 1024 * 1024),
        cost_estimate=pl.CostEstimate(flops=0, bytes_accessed=5_000_000, transcendentals=0),
        name="slice_columns",
    )(turn, *[weight] * NX)


def project_kernel(w_ref, a0_ref, a1_ref, a2_ref, a3_ref, out_ref):
    heads = jnp.concatenate([ref[...] for ref in (a0_ref, a1_ref, a2_ref, a3_ref)], axis=0)
    out_ref[...] = jnp.dot(w_ref[...], heads, preferred_element_type=jnp.float32).astype(jnp.bfloat16)


def project(weight, heads):
    rows = NZ * NY * HEAD
    return pl.pallas_call(
        project_kernel,
        grid=(TOK // CHUNK,),
        in_specs=[pl.BlockSpec((rows, NX * HEAD), lambda k: (0, 0))]
        + [pl.BlockSpec((HEAD, CHUNK), lambda k: (0, k))] * NX,
        out_specs=pl.BlockSpec((rows, CHUNK), lambda k: (0, k)),
        out_shape=jax.ShapeDtypeStruct((rows, TOK), jnp.bfloat16),
        compiler_params=pltpu.CompilerParams(vmem_limit_bytes=24 * 1024 * 1024),
        cost_estimate=pl.CostEstimate(flops=2_500_000_000, bytes_accessed=7_000_000, transcendentals=0),
        name="project",
    )(weight, *heads)


def spread_kernel(parts_ref, received_ref, up_ref, middle_ref, out_ref):
    total = received_ref[...].astype(jnp.float32)
    head_sum = parts_ref[0].astype(jnp.float32)
    for x in range(1, NZ * NY):
        head_sum += parts_ref[x].astype(jnp.float32)
    middle = (total + head_sum).astype(jnp.bfloat16)
    middle_ref[...] = middle
    middle_f = middle.astype(jnp.float32)
    squares = jnp.sum(middle_f * middle_f, axis=0, keepdims=True)
    high = squares.astype(jnp.bfloat16).astype(jnp.float32)
    low = squares - high
    rows = [high[:, k * 128 : (k + 1) * 128] for k in range(8)] + [low[:, k * 128 : (k + 1) * 128] for k in range(8)]
    tile = jnp.concatenate(rows + [jnp.zeros((8, 128), jnp.float32)], axis=0)
    out_ref[:, TOK:] = jnp.concatenate([tile] * BLOCKS, axis=0).astype(jnp.bfloat16)
    out_ref[:, :TOK] = jnp.dot(up_ref[...], middle, preferred_element_type=jnp.float32).astype(jnp.bfloat16)


def spread_call(parts, received, up):
    return pl.pallas_call(
        spread_kernel,
        out_shape=(
            jax.ShapeDtypeStruct((HEAD, TOK), jnp.bfloat16),
            jax.ShapeDtypeStruct((WIDE, TOK + EXTRA), jnp.bfloat16),
        ),
        compiler_params=pltpu.CompilerParams(vmem_limit_bytes=20 * 1024 * 1024),
        cost_estimate=pl.CostEstimate(flops=310_000_000, bytes_accessed=5_000_000, transcendentals=0),
        name="spread",
    )(parts, received, up)


def hidden_kernel(up_ref, down_ref, r_ref, out_ref):
    sums = jnp.sum(r_ref[:, TOK:].astype(jnp.float32).reshape(BLOCKS, PIECE, 128), axis=0)
    sums = sums[0:8] + sums[8:16]
    total = jnp.concatenate([sums[k : k + 1] for k in range(8)], axis=1)
    scaling = lax.rsqrt(total * (1.0 / D) + epsilon)
    for part in range(TOK // CHUNK):
        cols = slice(part * CHUNK, (part + 1) * CHUNK)
        pre = jnp.dot(up_ref[...], r_ref[:, cols], preferred_element_type=jnp.float32) * scaling[:, cols]
        hidden = 0.5 * pre * (1.0 + jnp.tanh(0.7978845608028654 * (pre + 0.044715 * (pre * pre * pre))))
        out_ref[:, cols] = jnp.dot(
            down_ref[...], hidden.astype(jnp.bfloat16), preferred_element_type=jnp.float32
        ).astype(jnp.bfloat16)


def hidden_call(up, down, pieces):
    return pl.pallas_call(
        hidden_kernel,
        out_shape=jax.ShapeDtypeStruct((WIDE, TOK), jnp.bfloat16),
        compiler_params=pltpu.CompilerParams(vmem_limit_bytes=24 * 1024 * 1024),
        cost_estimate=pl.CostEstimate(flops=2_500_000_000, bytes_accessed=6_000_000, transcendentals=1_000_000),
        name="hidden",
    )(up, down, pieces)


def final_kernel(down_ref, b_ref, middle_ref, out_ref):
    out = jnp.dot(down_ref[...], b_ref[...], preferred_element_type=jnp.float32)
    out_ref[...] = (middle_ref[...].astype(jnp.float32) + out).astype(jnp.bfloat16)


def final_call(down, pieces, middle):
    return pl.pallas_call(
        final_kernel,
        out_shape=jax.ShapeDtypeStruct((HEAD, TOK), jnp.bfloat16),
        compiler_params=pltpu.CompilerParams(vmem_limit_bytes=16 * 1024 * 1024),
        cost_estimate=pl.CostEstimate(flops=310_000_000, bytes_accessed=3_000_000, transcendentals=0),
        name="final",
    )(down, pieces, middle)


TENSOR = ("x", "z", "y")


def shift_pairs(count):
    devices = NX * NZ * NY
    return [(t, (t + devices) % (count * devices)) for t in range(count * devices)]


SWAP = [(0, 1), (1, 0)]


def around(axis, value, steps):
    return lax.ppermute(value, axis, [(at, (at + steps) % NX) for at in range(NX)])


def around_x(value, steps):
    return around("x", value, steps)


def spread_over(axis, value):
    return [value] + [around(axis, value, steps) for steps in (1, 3, 2)]


def in_order(pieces):
    return [pieces[0], pieces[1], pieces[3], pieces[2]]


def shards(
    incoming,
    scene_lengths,
    attn_gain,
    query_weight,
    key_weight,
    value_weight,
    output_weight,
    ffn_gain,
    up_first,
    up_second,
    down_first,
    down_second,
):
    everything = ("pipe",) + TENSOR
    count = lax.axis_size("pipe")
    received = lax.ppermute(incoming, everything, shift_pairs(count))
    place = lax.axis_index("z").astype(jnp.int32).reshape(1)
    weights = (attn_gain, query_weight, key_weight, value_weight)
    beside = half_weights(0, NX, 1 - place, *weights)
    ahead, _ = lax.optimization_barrier((received, beside))
    beside = lax.ppermute(beside, "z", SWAP)
    wide = jnp.broadcast_to(ahead[None, :, :HALF], (NX, HEAD, HALF))
    wide = lax.all_to_all(wide, "x", split_axis=0, concat_axis=0, tiled=True)
    tall = jnp.stack(in_order(spread_over("y", ahead[:, HALF:])))
    wide = in_order(spread_over("y", wide))
    tall = jnp.broadcast_to(tall[None], (NX, NY, HEAD, HALF))
    tall = lax.all_to_all(tall, "x", split_axis=0, concat_axis=0, tiled=True)
    corner = lax.axis_index("y").astype(jnp.int32).reshape(1)

    turn = lax.axis_index("x").astype(jnp.int32).reshape(1)
    tied = (ahead, *weights, output_weight, up_first, up_second, down_first, down_second, ffn_gain)
    tied = lax.optimization_barrier(tied)
    _, *weights, output_weight, up_first, up_second, down_first, down_second, ffn_gain = tied
    own_weights = half_weights(0, NX, place, *weights)
    columns = slice_columns(turn, output_weight)
    up_first = (up_first.reshape(HEAD, WIDE).T.astype(jnp.float32) * ffn_gain).astype(jnp.bfloat16)
    up_second = up_second.reshape(WIDE, WIDE).T
    down_first = down_first.reshape(WIDE, WIDE).T
    down_second = down_second.reshape(WIDE, HEAD).T
    tied = (beside, own_weights, columns, up_first, up_second, down_first, down_second)
    tied = lax.optimization_barrier(tied)
    beside, own_weights, columns, up_first, up_second, down_first, down_second = tied
    mark = arrival_mark(beside)

    crossed, crossed_values, squares = cross_projection(corner, beside, wide, tall, mark)
    came = lax.ppermute(crossed, "z", SWAP)
    came_values = lax.ppermute(crossed_values, "z", SWAP)
    _, own_weights, columns = lax.optimization_barrier((crossed, own_weights, columns))
    own = own_projection(corner, own_weights, wide, tall)
    blocks = [columns[0]] + [around_x(columns[k], k) for k in range(1, NX)]
    out_weight = jnp.concatenate(blocks, axis=0).T

    expo, rows = attention_weights(scene_lengths, own, came, squares)
    attended = mix_values(own, came_values, expo, rows)
    heads = [attended] + [around_x(attended, k) for k in range(1, NX)]
    partial = project(out_weight, heads)
    parts = lax.all_to_all(
        partial.reshape(NZ * NY, HEAD, TOK), ("z", "y"), split_axis=0, concat_axis=0, tiled=True
    )
    middle, spread = spread_call(parts, received, up_first)
    pieces = lax.all_to_all(
        spread.reshape(BLOCKS, PIECE, TOK + EXTRA), TENSOR, split_axis=0, concat_axis=0, tiled=True
    )
    mixed_back = hidden_call(up_second, down_first, pieces.reshape(WIDE, TOK + EXTRA))
    returned = lax.all_to_all(
        mixed_back.reshape(BLOCKS, PIECE, TOK), TENSOR, split_axis=0, concat_axis=0, tiled=True
    )
    return final_call(down_second, returned.reshape(WIDE, TOK), middle)


def solution(mesh):
    devices = mesh.devices
    finer = Mesh(devices.reshape(devices.shape[0], NX, NZ, NY), ("pipe",) + TENSOR)
    return jax.shard_map(
        shards,
        mesh=finer,
        in_specs=(
            P(TENSOR, "pipe"),
            P("pipe", None),
            P("pipe", None),
            P("pipe", TENSOR, None),
            P("pipe", TENSOR, None),
            P("pipe", TENSOR, None),
            P("pipe", TENSOR, None),
            P("pipe", TENSOR),
            P("pipe", TENSOR, None, None),
            P("pipe", TENSOR, None, None),
            P("pipe", TENSOR, None, None),
            P("pipe", TENSOR, None, None),
        ),
        out_specs=P(TENSOR, "pipe"),
        check_vma=False,
    )
```

```python
import functools

import jax
import jax.numpy as jnp
from jax import lax
from jax.experimental import pallas as pl
from jax.experimental.pallas import tpu as pltpu
from jax.sharding import Mesh, PartitionSpec as P

D = 6144
HEAD = 192
TOK = 1024
BLOCKS = 32
PIECE = 24
WIDE = 768
CHUNK = 256
NX, NZ, NY = 4, 2, 4
PART = NX // 2
EXTRA = 128
HALF = TOK // 2
MARK_FLOPS = 12_000_000_000

epsilon = 1e-06


def scale_kernel(half_ref, gain_ref, wq_ref, wk_ref, wv_ref, out_ref):
    gain = gain_ref[...]
    for part, ref in enumerate((wq_ref, wk_ref, wv_ref)):
        out_ref[0, part * HEAD : (part + 1) * HEAD, :] = (ref[0].astype(jnp.float32) * gain).astype(jnp.bfloat16)


def half_weights(first, count, half, gain, query_weight, key_weight, value_weight):
    weight_spec = pl.BlockSpec((1, HEAD, WIDE), lambda k, half_ref: (0, 0, 2 * (k + first) + half_ref[0]))
    return pl.pallas_call(
        scale_kernel,
        grid_spec=pltpu.PrefetchScalarGridSpec(
            num_scalar_prefetch=1,
            grid=(count,),
            in_specs=[
                pl.BlockSpec((1, WIDE), lambda k, half_ref: (0, 2 * (k + first) + half_ref[0])),
                weight_spec,
                weight_spec,
                weight_spec,
            ],
            out_specs=pl.BlockSpec((1, 3 * HEAD, WIDE), lambda k, half_ref: (k, 0, 0)),
        ),
        out_shape=jax.ShapeDtypeStruct((count, 3 * HEAD, WIDE), jnp.bfloat16),
        compiler_params=pltpu.CompilerParams(vmem_limit_bytes=58 * 1024 * 1024),
        cost_estimate=pl.CostEstimate(flops=0, bytes_accessed=7_000_000, transcendentals=0),
        name="half_weights",
    )(half, gain, query_weight, key_weight, value_weight)


def accumulate(product, acc_ref):
    @pl.when(pl.program_id(0) == 0)
    def _():
        acc_ref[...] = product

    @pl.when(pl.program_id(0) > 0)
    def _():
        acc_ref[...] += product


def block_copies(x, place_ref, wide_refs, tall_ref, g_buffer, sems, first=0):
    copies = []
    for j in range(NY):
        rows = pl.ds(pl.multiple_of(lax.rem(place_ref[0] + NY - j, NY) * HEAD, HEAD), HEAD)
        copies.append(pltpu.make_async_copy(wide_refs[j].at[x], g_buffer.at[x - first, rows, pl.ds(0, HALF)], sems.at[x, j]))
        copies.append(
            pltpu.make_async_copy(tall_ref.at[x, j], g_buffer.at[x - first, rows, pl.ds(HALF, HALF)], sems.at[x, NY + j])
        )
    return x, copies


def start_all(copies):
    for copy in copies:
        copy.start()


def wait_all(copies):
    for copy in copies:
        copy.wait()


def token_squares(block):
    block_f = block.astype(jnp.float32)
    return jnp.sum((block_f * block_f).reshape(WIDE // 8, 8, TOK), axis=0)


def early_kernel(place_ref, w_ref, *refs):
    wide_refs, tall_ref = refs[:NY], refs[NY]
    out_ref, squares_ref, w_buffer, g_buffer, w_sem, g_sems = refs[NY + 2 :]
    weights = pltpu.make_async_copy(w_ref, w_buffer, w_sem)
    weights.start()
    steps = [block_copies(x, place_ref, wide_refs, tall_ref, g_buffer, g_sems) for x in range(PART)]
    for _, copies in steps:
        start_all(copies)
    weights.wait()
    for x, copies in steps:
        wait_all(copies)
        squares = token_squares(g_buffer[x])
        squares_ref[...] = squares if x == 0 else squares_ref[...] + squares
        for part in range(2):
            cols = slice(part * HALF, (part + 1) * HALF)
            product = jnp.dot(w_buffer[x], g_buffer[x, :, cols], preferred_element_type=jnp.float32)
            out_ref[:, cols] = product if x == 0 else out_ref[:, cols] + product


def early_projection(place, weights, wide, tall, mark):
    return pl.pallas_call(
        early_kernel,
        in_specs=[pl.BlockSpec(memory_space=pltpu.SMEM)] + [pl.BlockSpec(memory_space=pl.ANY)] * (3 + NY),
        out_shape=(
            jax.ShapeDtypeStruct((3 * HEAD, TOK), jnp.float32),
            jax.ShapeDtypeStruct((8, TOK), jnp.float32),
        ),
        scratch_shapes=[
            pltpu.VMEM((PART, 3 * HEAD, WIDE), jnp.bfloat16),
            pltpu.VMEM((PART, WIDE, TOK), jnp.bfloat16),
            pltpu.SemaphoreType.DMA,
            pltpu.SemaphoreType.DMA((NX, 2 * NY)),
        ],
        compiler_params=pltpu.CompilerParams(vmem_limit_bytes=32 * 1024 * 1024),
        cost_estimate=pl.CostEstimate(flops=1_000_000, bytes_accessed=10_000, transcendentals=0),
        name="early_projection",
    )(place, weights, *wide, tall, mark)


def cross_kernel(place_ref, w_ref, *refs):
    wide_refs, tall_ref, early_ref, early_squares_ref = refs[:NY], *refs[NY : NY + 3]
    out_ref, values_ref, squares_ref, w_buffer, g_buffer, acc_ref, w_sem, g_sems, acc_sem = refs[NY + 3 :]
    weights = pltpu.make_async_copy(w_ref, w_buffer, w_sem)
    weights.start()
    later = range(PART, NX)
    steps = [block_copies(x, place_ref, wide_refs, tall_ref, g_buffer, g_sems, PART) for x in later]
    for _, copies in steps:
        start_all(copies)
    early = pltpu.make_async_copy(early_ref, acc_ref, acc_sem)
    early.start()
    squares_ref[...] = early_squares_ref[...]
    weights.wait()
    for x, copies in steps:
        wait_all(copies)
        squares_ref[...] += token_squares(g_buffer[x - PART])
        if x == PART:
            early.wait()
        for part in range(2):
            cols = slice(part * HALF, (part + 1) * HALF)
            product = jnp.dot(w_buffer[x - PART], g_buffer[x - PART, :, cols], preferred_element_type=jnp.float32)
            product = acc_ref[:, cols] + product
            if x < NX - 1:
                acc_ref[:, cols] = product
            else:
                out_ref[: 2 * HEAD, cols] = product[: 2 * HEAD].astype(jnp.bfloat16)
                values_ref[:, cols] = product[2 * HEAD :].astype(jnp.bfloat16)
    total = jnp.sum(squares_ref[...], axis=0, keepdims=True)
    high = total.astype(jnp.bfloat16).astype(jnp.float32)
    tail = jnp.concatenate([high, total - high, jnp.zeros((14, TOK), jnp.float32)], axis=0)
    out_ref[2 * HEAD :, :] = tail.astype(jnp.bfloat16)


def cross_projection(place, weights, wide, tall, early, early_squares):
    in_any = pl.BlockSpec(memory_space=pl.ANY)
    return pl.pallas_call(
        cross_kernel,
        in_specs=[pl.BlockSpec(memory_space=pltpu.SMEM)]
        + [in_any] * (3 + NY)
        + [pl.BlockSpec(memory_space=pltpu.VMEM)],
        out_shape=(
            jax.ShapeDtypeStruct((2 * HEAD + 16, TOK), jnp.bfloat16),
            jax.ShapeDtypeStruct((HEAD, TOK), jnp.bfloat16),
            jax.ShapeDtypeStruct((8, TOK), jnp.float32),
        ),
        scratch_shapes=[
            pltpu.VMEM((NX - PART, 3 * HEAD, WIDE), jnp.bfloat16),
            pltpu.VMEM((NX - PART, WIDE, TOK), jnp.bfloat16),
            pltpu.VMEM((3 * HEAD, TOK), jnp.float32),
            pltpu.SemaphoreType.DMA,
            pltpu.SemaphoreType.DMA((NX, 2 * NY)),
            pltpu.SemaphoreType.DMA,
        ],
        compiler_params=pltpu.CompilerParams(vmem_limit_bytes=32 * 1024 * 1024),
        cost_estimate=pl.CostEstimate(flops=1_000_000, bytes_accessed=10_000, transcendentals=0),
        name="cross_projection",
    )(place, weights, *wide, tall, early, early_squares)


def own_kernel(place_ref, w_ref, *refs):
    wide_refs, tall_ref = refs[:NY], refs[NY]
    out_ref, w_buffer, g_buffer, w_sem, g_sems = refs[NY + 1 :]
    weights = pltpu.make_async_copy(w_ref, w_buffer, w_sem)
    weights.start()
    steps = [block_copies(step, place_ref, wide_refs, tall_ref, g_buffer, g_sems) for step in range(NX)]
    for _, copies in steps:
        for copy in copies:
            copy.start()
    weights.wait()
    for step, (x, copies) in enumerate(steps):
        for copy in copies:
            copy.wait()
        for part in range(2):
            cols = slice(part * HALF, (part + 1) * HALF)
            product = jnp.dot(w_buffer[x], g_buffer[x, :, cols], preferred_element_type=jnp.float32)
            out_ref[:, cols] = product if step == 0 else out_ref[:, cols] + product


def own_projection(place, weights, wide, tall):
    return pl.pallas_call(
        own_kernel,
        in_specs=[pl.BlockSpec(memory_space=pltpu.SMEM)] + [pl.BlockSpec(memory_space=pl.ANY)] * (2 + NY),
        out_shape=jax.ShapeDtypeStruct((3 * HEAD, TOK), jnp.float32),
        scratch_shapes=[
            pltpu.VMEM((NX, 3 * HEAD, WIDE), jnp.bfloat16),
            pltpu.VMEM((NX, WIDE, TOK), jnp.bfloat16),
            pltpu.SemaphoreType.DMA,
            pltpu.SemaphoreType.DMA((NX, 2 * NY)),
        ],
        compiler_params=pltpu.CompilerParams(vmem_limit_bytes=32 * 1024 * 1024),
        cost_estimate=pl.CostEstimate(flops=1_000_000, bytes_accessed=10_000, transcendentals=0),
        name="own_projection",
    )(place, weights, *wide, tall)


def mark_kernel(w_ref, out_ref):
    out_ref[...] = jnp.zeros_like(out_ref)


def arrival_mark(weights):
    return pl.pallas_call(
        mark_kernel,
        in_specs=[pl.BlockSpec(memory_space=pl.ANY)],
        out_shape=jax.ShapeDtypeStruct((8, 128), jnp.float32),
        cost_estimate=pl.CostEstimate(flops=MARK_FLOPS, bytes_accessed=1000, transcendentals=0),
        name="arrival_mark",
    )(weights)


def scaling_of(squares_ref, tail):
    tail = tail.astype(jnp.float32)
    total = jnp.sum(squares_ref[...], axis=0, keepdims=True) + tail[0:1] + tail[1:2]
    return lax.rsqrt(total * (1.0 / D) + epsilon)


def weigh_kernel(lengths_ref, own_ref, came_ref, squares_ref, expo_ref, rows_ref):
    scaling = scaling_of(squares_ref, came_ref[2 * HEAD :, :])
    both = (own_ref[: 2 * HEAD, :] + came_ref[: 2 * HEAD, :].astype(jnp.float32)) * scaling
    query = both[:HEAD, :].astype(jnp.bfloat16)
    keys = both[HEAD:, :].astype(jnp.bfloat16).T
    rows_ref[0:1, :] = scaling
    first = lengths_ref[0, 0]
    second = first + lengths_ref[0, 1]
    third = second + lengths_ref[0, 2]

    def scene(position):
        return (
            (position >= first).astype(jnp.int32)
            + (position >= second).astype(jnp.int32)
            + (position >= third).astype(jnp.int32)
        )

    key_scene = scene(lax.broadcasted_iota(jnp.int32, (TOK, 1), 0))
    for part in range(TOK // CHUNK):
        cols = slice(part * CHUNK, (part + 1) * CHUNK)
        query_scene = scene(lax.broadcasted_iota(jnp.int32, (1, CHUNK), 1) + part * CHUNK)
        scores = jnp.dot(keys, query[:, cols], preferred_element_type=jnp.float32)
        scores = jnp.where(key_scene == query_scene, scores * HEAD ** (-0.5), -jnp.inf)
        expo = jnp.exp(scores - jnp.max(scores, axis=0, keepdims=True))
        rows_ref[1:2, cols] = 1.0 / jnp.sum(expo, axis=0, keepdims=True)
        expo_ref[:, cols] = expo.astype(jnp.bfloat16)


def attention_weights(lengths, own, came, squares):
    whole = pl.BlockSpec(memory_space=pltpu.VMEM)
    return pl.pallas_call(
        weigh_kernel,
        in_specs=[pl.BlockSpec(memory_space=pltpu.SMEM)] + [whole] * 3,
        out_shape=(
            jax.ShapeDtypeStruct((TOK, TOK), jnp.bfloat16),
            jax.ShapeDtypeStruct((2, TOK), jnp.float32),
        ),
        compiler_params=pltpu.CompilerParams(vmem_limit_bytes=24 * 1024 * 1024),
        cost_estimate=pl.CostEstimate(flops=500_000_000, bytes_accessed=6_000_000, transcendentals=1_000_000),
        name="attention_weights",
    )(lengths, own, came, squares)


def mix_kernel(own_ref, came_ref, expo_ref, rows_ref, out_ref):
    values = (own_ref[2 * HEAD :, :] + came_ref[...].astype(jnp.float32)) * rows_ref[0:1, :]
    values = values.astype(jnp.bfloat16)
    for part in range(TOK // CHUNK):
        cols = slice(part * CHUNK, (part + 1) * CHUNK)
        mixed = jnp.dot(values, expo_ref[:, cols], preferred_element_type=jnp.float32)
        mixed = (mixed * rows_ref[1:2, cols]).astype(jnp.bfloat16)
        out_ref[:, cols] = mixed


def mix_values(own, came, expo, rows):
    return pl.pallas_call(
        mix_kernel,
        out_shape=jax.ShapeDtypeStruct((HEAD, TOK), jnp.bfloat16),
        compiler_params=pltpu.CompilerParams(vmem_limit_bytes=20 * 1024 * 1024),
        cost_estimate=pl.CostEstimate(flops=400_000_000, bytes_accessed=7_000_000, transcendentals=0),
        name="mix_values",
    )(own, came, expo, rows)


def copy_kernel(turn_ref, *refs):
    for in_ref, out_ref in zip(refs[:NX], refs[NX:]):
        out_ref[...] = in_ref[0]


def slice_columns(turn, weight):
    width = NZ * NY * HEAD

    def column_spec(k):
        return pl.BlockSpec((1, HEAD, width), lambda i, turn_ref: (0, 0, (turn_ref[0] + k) % NX))

    return pl.pallas_call(
        copy_kernel,
        grid_spec=pltpu.PrefetchScalarGridSpec(
            num_scalar_prefetch=1,
            grid=(1,),
            in_specs=[column_spec(k) for k in range(NX)],
            out_specs=[pl.BlockSpec((HEAD, width), lambda i, turn_ref: (0, 0))] * NX,
        ),
        out_shape=[jax.ShapeDtypeStruct((HEAD, width), jnp.bfloat16)] * NX,
        compiler_params=pltpu.CompilerParams(vmem_limit_bytes=48 * 1024 * 1024),
        cost_estimate=pl.CostEstimate(flops=0, bytes_accessed=5_000_000, transcendentals=0),
        name="slice_columns",
    )(turn, *[weight] * NX)


def project_kernel(w_ref, a0_ref, a1_ref, a2_ref, a3_ref, out_ref):
    heads = jnp.concatenate([ref[...] for ref in (a0_ref, a1_ref, a2_ref, a3_ref)], axis=0)
    out_ref[...] = jnp.dot(w_ref[...], heads, preferred_element_type=jnp.float32).astype(jnp.bfloat16)


def project(weight, heads):
    rows = NZ * NY * HEAD
    return pl.pallas_call(
        project_kernel,
        grid=(TOK // CHUNK,),
        in_specs=[pl.BlockSpec((rows, NX * HEAD), lambda k: (0, 0))]
        + [pl.BlockSpec((HEAD, CHUNK), lambda k: (0, k))] * NX,
        out_specs=pl.BlockSpec((rows, CHUNK), lambda k: (0, k)),
        out_shape=jax.ShapeDtypeStruct((rows, TOK), jnp.bfloat16),
        compiler_params=pltpu.CompilerParams(vmem_limit_bytes=24 * 1024 * 1024),
        cost_estimate=pl.CostEstimate(flops=2_500_000_000, bytes_accessed=7_000_000, transcendentals=0),
        name="project",
    )(weight, *heads)


def spread_kernel(parts_ref, received_ref, up_ref, middle_ref, out_ref):
    total = received_ref[...].astype(jnp.float32)
    head_sum = parts_ref[0].astype(jnp.float32)
    for x in range(1, NZ * NY):
        head_sum += parts_ref[x].astype(jnp.float32)
    middle = (total + head_sum).astype(jnp.bfloat16)
    middle_ref[...] = middle
    middle_f = middle.astype(jnp.float32)
    squares = jnp.sum(middle_f * middle_f, axis=0, keepdims=True)
    high = squares.astype(jnp.bfloat16).astype(jnp.float32)
    low = squares - high
    rows = [high[:, k * 128 : (k + 1) * 128] for k in range(8)] + [low[:, k * 128 : (k + 1) * 128] for k in range(8)]
    tile = jnp.concatenate(rows + [jnp.zeros((8, 128), jnp.float32)], axis=0)
    out_ref[:, TOK:] = jnp.concatenate([tile] * BLOCKS, axis=0).astype(jnp.bfloat16)
    out_ref[:, :TOK] = jnp.dot(up_ref[...], middle, preferred_element_type=jnp.float32).astype(jnp.bfloat16)


def spread_call(parts, received, up):
    return pl.pallas_call(
        spread_kernel,
        out_shape=(
            jax.ShapeDtypeStruct((HEAD, TOK), jnp.bfloat16),
            jax.ShapeDtypeStruct((WIDE, TOK + EXTRA), jnp.bfloat16),
        ),
        compiler_params=pltpu.CompilerParams(vmem_limit_bytes=20 * 1024 * 1024),
        cost_estimate=pl.CostEstimate(flops=310_000_000, bytes_accessed=5_000_000, transcendentals=0),
        name="spread",
    )(parts, received, up)


def hidden_kernel(up_ref, down_ref, r_ref, out_ref):
    sums = jnp.sum(r_ref[:, TOK:].astype(jnp.float32).reshape(BLOCKS, PIECE, 128), axis=0)
    sums = sums[0:8] + sums[8:16]
    total = jnp.concatenate([sums[k : k + 1] for k in range(8)], axis=1)
    scaling = lax.rsqrt(total * (1.0 / D) + epsilon)
    for part in range(TOK // CHUNK):
        cols = slice(part * CHUNK, (part + 1) * CHUNK)
        pre = jnp.dot(up_ref[...], r_ref[:, cols], preferred_element_type=jnp.float32) * scaling[:, cols]
        hidden = 0.5 * pre * (1.0 + jnp.tanh(0.7978845608028654 * (pre + 0.044715 * (pre * pre * pre))))
        out_ref[:, cols] = jnp.dot(
            down_ref[...], hidden.astype(jnp.bfloat16), preferred_element_type=jnp.float32
        ).astype(jnp.bfloat16)


def hidden_call(up, down, pieces):
    return pl.pallas_call(
        hidden_kernel,
        out_shape=jax.ShapeDtypeStruct((WIDE, TOK), jnp.bfloat16),
        compiler_params=pltpu.CompilerParams(vmem_limit_bytes=24 * 1024 * 1024),
        cost_estimate=pl.CostEstimate(flops=2_500_000_000, bytes_accessed=6_000_000, transcendentals=1_000_000),
        name="hidden",
    )(up, down, pieces)


def final_kernel(down_ref, b_ref, middle_ref, out_ref):
    out = jnp.dot(down_ref[...], b_ref[...], preferred_element_type=jnp.float32)
    out_ref[...] = (middle_ref[...].astype(jnp.float32) + out).astype(jnp.bfloat16)


def final_call(down, pieces, middle):
    return pl.pallas_call(
        final_kernel,
        out_shape=jax.ShapeDtypeStruct((HEAD, TOK), jnp.bfloat16),
        compiler_params=pltpu.CompilerParams(vmem_limit_bytes=16 * 1024 * 1024),
        cost_estimate=pl.CostEstimate(flops=310_000_000, bytes_accessed=3_000_000, transcendentals=0),
        name="final",
    )(down, pieces, middle)


TENSOR = ("x", "z", "y")


def shift_pairs(count):
    devices = NX * NZ * NY
    return [(t, (t + devices) % (count * devices)) for t in range(count * devices)]


SWAP = [(0, 1), (1, 0)]


def around(axis, value, steps):
    return lax.ppermute(value, axis, [(at, (at + steps) % NX) for at in range(NX)])


def around_x(value, steps):
    return around("x", value, steps)


def spread_over(axis, value):
    return [value] + [around(axis, value, steps) for steps in (1, 3, 2)]


def in_order(pieces):
    return [pieces[0], pieces[1], pieces[3], pieces[2]]


def shards(
    incoming,
    scene_lengths,
    attn_gain,
    query_weight,
    key_weight,
    value_weight,
    output_weight,
    ffn_gain,
    up_first,
    up_second,
    down_first,
    down_second,
):
    everything = ("pipe",) + TENSOR
    count = lax.axis_size("pipe")
    received = lax.ppermute(incoming, everything, shift_pairs(count))
    place = lax.axis_index("z").astype(jnp.int32).reshape(1)
    weights = (attn_gain, query_weight, key_weight, value_weight)
    first = half_weights(0, PART, 1 - place, *weights)
    second = half_weights(PART, NX - PART, 1 - place, *weights)
    ahead, _, _ = lax.optimization_barrier((received, first, second))
    first = lax.ppermute(first, "z", SWAP)
    second = lax.ppermute(second, "z", SWAP)
    wide = jnp.broadcast_to(ahead[None, :, :HALF], (NX, HEAD, HALF))
    wide = lax.all_to_all(wide, "x", split_axis=0, concat_axis=0, tiled=True)
    tall = jnp.stack(in_order(spread_over("y", ahead[:, HALF:])))
    wide = in_order(spread_over("y", wide))
    tall = jnp.broadcast_to(tall[None], (NX, NY, HEAD, HALF))
    tall = lax.all_to_all(tall, "x", split_axis=0, concat_axis=0, tiled=True)
    corner = lax.axis_index("y").astype(jnp.int32).reshape(1)

    turn = lax.axis_index("x").astype(jnp.int32).reshape(1)
    tied = (first, *weights, output_weight, up_first, up_second, down_first, down_second, ffn_gain)
    tied = lax.optimization_barrier(tied)
    first, *weights, output_weight, up_first, up_second, down_first, down_second, ffn_gain = tied
    own_weights = half_weights(0, NX, place, *weights)
    columns = slice_columns(turn, output_weight)
    up_first = (up_first.reshape(HEAD, WIDE).T.astype(jnp.float32) * ffn_gain).astype(jnp.bfloat16)
    up_second = up_second.reshape(WIDE, WIDE).T
    down_first = down_first.reshape(WIDE, WIDE).T
    down_second = down_second.reshape(WIDE, HEAD).T
    tied = (first, own_weights, columns, up_first, up_second, down_first, down_second)
    tied = lax.optimization_barrier(tied)
    first, own_weights, columns, up_first, up_second, down_first, down_second = tied
    mark = arrival_mark(first)

    early = early_projection(corner, first, wide, tall, mark)
    second, early = lax.optimization_barrier((second, early))
    crossed, crossed_values, squares = cross_projection(corner, second, wide, tall, *early)
    came = lax.ppermute(crossed, "z", SWAP)
    came_values = lax.ppermute(crossed_values, "z", SWAP)
    _, own_weights, columns = lax.optimization_barrier((crossed, own_weights, columns))
    own = own_projection(corner, own_weights, wide, tall)
    blocks = [columns[0]] + [around_x(columns[k], k) for k in range(1, NX)]
    out_weight = jnp.concatenate(blocks, axis=0).T

    expo, rows = attention_weights(scene_lengths, own, came, squares)
    attended = mix_values(own, came_values, expo, rows)
    heads = [attended] + [around_x(attended, k) for k in range(1, NX)]
    partial = project(out_weight, heads)
    parts = lax.all_to_all(
        partial.reshape(NZ * NY, HEAD, TOK), ("z", "y"), split_axis=0, concat_axis=0, tiled=True
    )
    middle, spread = spread_call(parts, received, up_first)
    pieces = lax.all_to_all(
        spread.reshape(BLOCKS, PIECE, TOK + EXTRA), TENSOR, split_axis=0, concat_axis=0, tiled=True
    )
    mixed_back = hidden_call(up_second, down_first, pieces.reshape(WIDE, TOK + EXTRA))
    returned = lax.all_to_all(
        mixed_back.reshape(BLOCKS, PIECE, TOK), TENSOR, split_axis=0, concat_axis=0, tiled=True
    )
    return final_call(down_second, returned.reshape(WIDE, TOK), middle)


def solution(mesh):
    devices = mesh.devices
    finer = Mesh(devices.reshape(devices.shape[0], NX, NZ, NY), ("pipe",) + TENSOR)
    return jax.shard_map(
        shards,
        mesh=finer,
        in_specs=(
            P(TENSOR, "pipe"),
            P("pipe", None),
            P("pipe", None),
            P("pipe", TENSOR, None),
            P("pipe", TENSOR, None),
            P("pipe", TENSOR, None),
            P("pipe", TENSOR, None),
            P("pipe", TENSOR),
            P("pipe", TENSOR, None, None),
            P("pipe", TENSOR, None, None),
            P("pipe", TENSOR, None, None),
            P("pipe", TENSOR, None, None),
        ),
        out_specs=P(TENSOR, "pipe"),
        check_vma=False,
    )
```

```python
import functools

import jax
import jax.numpy as jnp
from jax import lax
from jax.experimental import pallas as pl
from jax.experimental.pallas import tpu as pltpu
from jax.sharding import Mesh, PartitionSpec as P

D = 6144
HEAD = 192
TOK = 1024
BLOCKS = 32
PIECE = 24
WIDE = 768
CHUNK = 256
NX, NZ, NY = 4, 2, 4
PART = NX // 2
EXTRA = 128
HALF = TOK // 2
MARK_FLOPS = 12_000_000_000

epsilon = 1e-06


def scale_kernel(half_ref, gain_ref, wq_ref, wk_ref, wv_ref, out_ref):
    gain = gain_ref[...]
    for part, ref in enumerate((wq_ref, wk_ref, wv_ref)):
        out_ref[0, part * HEAD : (part + 1) * HEAD, :] = (ref[0].astype(jnp.float32) * gain).astype(jnp.bfloat16)


def half_weights(first, count, half, gain, query_weight, key_weight, value_weight):
    weight_spec = pl.BlockSpec((1, HEAD, WIDE), lambda k, half_ref: (0, 0, 2 * (k + first) + half_ref[0]))
    return pl.pallas_call(
        scale_kernel,
        grid_spec=pltpu.PrefetchScalarGridSpec(
            num_scalar_prefetch=1,
            grid=(count,),
            in_specs=[
                pl.BlockSpec((1, WIDE), lambda k, half_ref: (0, 2 * (k + first) + half_ref[0])),
                weight_spec,
                weight_spec,
                weight_spec,
            ],
            out_specs=pl.BlockSpec((1, 3 * HEAD, WIDE), lambda k, half_ref: (k, 0, 0)),
        ),
        out_shape=jax.ShapeDtypeStruct((count, 3 * HEAD, WIDE), jnp.bfloat16),
        compiler_params=pltpu.CompilerParams(vmem_limit_bytes=58 * 1024 * 1024),
        cost_estimate=pl.CostEstimate(flops=0, bytes_accessed=7_000_000, transcendentals=0),
        name="half_weights",
    )(half, gain, query_weight, key_weight, value_weight)


def accumulate(product, acc_ref):
    @pl.when(pl.program_id(0) == 0)
    def _():
        acc_ref[...] = product

    @pl.when(pl.program_id(0) > 0)
    def _():
        acc_ref[...] += product


def block_copies(x, place_ref, wide_refs, tall_ref, g_buffer, sems, first=0):
    copies = []
    for j in range(NY):
        rows = pl.ds(pl.multiple_of(lax.rem(place_ref[0] + NY - j, NY) * HEAD, HEAD), HEAD)
        copies.append(pltpu.make_async_copy(wide_refs[j].at[x], g_buffer.at[x - first, rows, pl.ds(0, HALF)], sems.at[x, j]))
        copies.append(
            pltpu.make_async_copy(tall_ref.at[x, j], g_buffer.at[x - first, rows, pl.ds(HALF, HALF)], sems.at[x, NY + j])
        )
    return x, copies


def start_all(copies):
    for copy in copies:
        copy.start()


def wait_all(copies):
    for copy in copies:
        copy.wait()


def token_squares(block):
    block_f = block.astype(jnp.float32)
    return jnp.sum((block_f * block_f).reshape(WIDE // 8, 8, TOK), axis=0)


def early_kernel(place_ref, w_ref, *refs):
    wide_refs, tall_ref = refs[:NY], refs[NY]
    out_ref, squares_ref, w_buffer, g_buffer, w_sem, g_sems = refs[NY + 2 :]
    weights = pltpu.make_async_copy(w_ref, w_buffer, w_sem)
    weights.start()
    steps = [block_copies(x, place_ref, wide_refs, tall_ref, g_buffer, g_sems) for x in range(PART)]
    for _, copies in steps:
        start_all(copies)
    weights.wait()
    for x, copies in steps:
        wait_all(copies)
        squares = token_squares(g_buffer[x])
        squares_ref[...] = squares if x == 0 else squares_ref[...] + squares
        for part in range(2):
            cols = slice(part * HALF, (part + 1) * HALF)
            product = jnp.dot(w_buffer[x], g_buffer[x, :, cols], preferred_element_type=jnp.float32)
            out_ref[:, cols] = product if x == 0 else out_ref[:, cols] + product


def early_projection(place, weights, wide, tall, mark):
    return pl.pallas_call(
        early_kernel,
        in_specs=[pl.BlockSpec(memory_space=pltpu.SMEM)] + [pl.BlockSpec(memory_space=pl.ANY)] * (3 + NY),
        out_shape=(
            jax.ShapeDtypeStruct((3 * HEAD, TOK), jnp.float32),
            jax.ShapeDtypeStruct((8, TOK), jnp.float32),
        ),
        scratch_shapes=[
            pltpu.VMEM((PART, 3 * HEAD, WIDE), jnp.bfloat16),
            pltpu.VMEM((PART, WIDE, TOK), jnp.bfloat16),
            pltpu.SemaphoreType.DMA,
            pltpu.SemaphoreType.DMA((NX, 2 * NY)),
        ],
        compiler_params=pltpu.CompilerParams(vmem_limit_bytes=32 * 1024 * 1024),
        cost_estimate=pl.CostEstimate(flops=1_000_000, bytes_accessed=10_000, transcendentals=0),
        name="early_projection",
    )(place, weights, *wide, tall, mark)


def cross_kernel(place_ref, w_ref, *refs):
    wide_refs, tall_ref, early_ref, early_squares_ref = refs[:NY], *refs[NY : NY + 3]
    out_ref, values_ref, squares_ref, w_buffer, g_buffer, acc_ref, w_sem, g_sems, acc_sem = refs[NY + 3 :]
    weights = pltpu.make_async_copy(w_ref, w_buffer, w_sem)
    weights.start()
    later = range(PART, NX)
    steps = [block_copies(x, place_ref, wide_refs, tall_ref, g_buffer, g_sems, PART) for x in later]
    for _, copies in steps:
        start_all(copies)
    early = pltpu.make_async_copy(early_ref, acc_ref, acc_sem)
    early.start()
    squares_ref[...] = early_squares_ref[...]
    weights.wait()
    for x, copies in steps:
        wait_all(copies)
        squares_ref[...] += token_squares(g_buffer[x - PART])
        if x == PART:
            early.wait()
        for part in range(2):
            cols = slice(part * HALF, (part + 1) * HALF)
            product = jnp.dot(w_buffer[x - PART], g_buffer[x - PART, :, cols], preferred_element_type=jnp.float32)
            product = acc_ref[:, cols] + product
            if x < NX - 1:
                acc_ref[:, cols] = product
            else:
                out_ref[: 2 * HEAD, cols] = product[: 2 * HEAD].astype(jnp.bfloat16)
                values_ref[:, cols] = product[2 * HEAD :].astype(jnp.bfloat16)
    total = jnp.sum(squares_ref[...], axis=0, keepdims=True)
    high = total.astype(jnp.bfloat16).astype(jnp.float32)
    tail = jnp.concatenate([high, total - high, jnp.zeros((14, TOK), jnp.float32)], axis=0)
    out_ref[2 * HEAD :, :] = tail.astype(jnp.bfloat16)


def cross_projection(place, weights, wide, tall, early, early_squares):
    in_any = pl.BlockSpec(memory_space=pl.ANY)
    return pl.pallas_call(
        cross_kernel,
        in_specs=[pl.BlockSpec(memory_space=pltpu.SMEM)]
        + [in_any] * (3 + NY)
        + [pl.BlockSpec(memory_space=pltpu.VMEM)],
        out_shape=(
            jax.ShapeDtypeStruct((2 * HEAD + 16, TOK), jnp.bfloat16),
            jax.ShapeDtypeStruct((HEAD, TOK), jnp.bfloat16),
            jax.ShapeDtypeStruct((8, TOK), jnp.float32),
        ),
        scratch_shapes=[
            pltpu.VMEM((NX - PART, 3 * HEAD, WIDE), jnp.bfloat16),
            pltpu.VMEM((NX - PART, WIDE, TOK), jnp.bfloat16),
            pltpu.VMEM((3 * HEAD, TOK), jnp.float32),
            pltpu.SemaphoreType.DMA,
            pltpu.SemaphoreType.DMA((NX, 2 * NY)),
            pltpu.SemaphoreType.DMA,
        ],
        compiler_params=pltpu.CompilerParams(vmem_limit_bytes=32 * 1024 * 1024),
        cost_estimate=pl.CostEstimate(flops=1_000_000, bytes_accessed=10_000, transcendentals=0),
        name="cross_projection",
    )(place, weights, *wide, tall, early, early_squares)


def own_kernel(place_ref, w_ref, *refs):
    wide_refs, tall_ref = refs[:NY], refs[NY]
    out_ref, w_buffer, g_buffer, w_sem, g_sems = refs[NY + 1 :]
    weights = pltpu.make_async_copy(w_ref, w_buffer, w_sem)
    weights.start()
    steps = [block_copies(step, place_ref, wide_refs, tall_ref, g_buffer, g_sems) for step in range(NX)]
    for _, copies in steps:
        for copy in copies:
            copy.start()
    weights.wait()
    for step, (x, copies) in enumerate(steps):
        for copy in copies:
            copy.wait()
        for part in range(2):
            cols = slice(part * HALF, (part + 1) * HALF)
            product = jnp.dot(w_buffer[x], g_buffer[x, :, cols], preferred_element_type=jnp.float32)
            out_ref[:, cols] = product if step == 0 else out_ref[:, cols] + product


def own_projection(place, weights, wide, tall):
    return pl.pallas_call(
        own_kernel,
        in_specs=[pl.BlockSpec(memory_space=pltpu.SMEM)] + [pl.BlockSpec(memory_space=pl.ANY)] * (2 + NY),
        out_shape=jax.ShapeDtypeStruct((3 * HEAD, TOK), jnp.float32),
        scratch_shapes=[
            pltpu.VMEM((NX, 3 * HEAD, WIDE), jnp.bfloat16),
            pltpu.VMEM((NX, WIDE, TOK), jnp.bfloat16),
            pltpu.SemaphoreType.DMA,
            pltpu.SemaphoreType.DMA((NX, 2 * NY)),
        ],
        compiler_params=pltpu.CompilerParams(vmem_limit_bytes=32 * 1024 * 1024),
        cost_estimate=pl.CostEstimate(flops=1_000_000, bytes_accessed=10_000, transcendentals=0),
        name="own_projection",
    )(place, weights, *wide, tall)


def mark_kernel(w_ref, out_ref):
    out_ref[...] = jnp.zeros_like(out_ref)


def arrival_mark(weights):
    return pl.pallas_call(
        mark_kernel,
        in_specs=[pl.BlockSpec(memory_space=pl.ANY)],
        out_shape=jax.ShapeDtypeStruct((8, 128), jnp.float32),
        cost_estimate=pl.CostEstimate(flops=MARK_FLOPS, bytes_accessed=1000, transcendentals=0),
        name="arrival_mark",
    )(weights)


def scaling_of(squares_ref, tail):
    tail = tail.astype(jnp.float32)
    total = jnp.sum(squares_ref[...], axis=0, keepdims=True) + tail[0:1] + tail[1:2]
    return lax.rsqrt(total * (1.0 / D) + epsilon)


def weigh_kernel(lengths_ref, own_ref, came_ref, squares_ref, expo_ref, rows_ref):
    scaling = scaling_of(squares_ref, came_ref[2 * HEAD :, :])
    both = (own_ref[: 2 * HEAD, :] + came_ref[: 2 * HEAD, :].astype(jnp.float32)) * scaling
    query = both[:HEAD, :].astype(jnp.bfloat16)
    keys = both[HEAD:, :].astype(jnp.bfloat16).T
    rows_ref[0:1, :] = scaling
    first = lengths_ref[0, 0]
    second = first + lengths_ref[0, 1]
    third = second + lengths_ref[0, 2]

    def scene(position):
        return (
            (position >= first).astype(jnp.int32)
            + (position >= second).astype(jnp.int32)
            + (position >= third).astype(jnp.int32)
        )

    key_scene = scene(lax.broadcasted_iota(jnp.int32, (TOK, 1), 0))
    for part in range(TOK // CHUNK):
        cols = slice(part * CHUNK, (part + 1) * CHUNK)
        query_scene = scene(lax.broadcasted_iota(jnp.int32, (1, CHUNK), 1) + part * CHUNK)
        scores = jnp.dot(keys, query[:, cols], preferred_element_type=jnp.float32)
        scores = jnp.where(key_scene == query_scene, scores * HEAD ** (-0.5), -jnp.inf)
        expo = jnp.exp(scores - jnp.max(scores, axis=0, keepdims=True))
        rows_ref[1:2, cols] = 1.0 / jnp.sum(expo, axis=0, keepdims=True)
        expo_ref[:, cols] = expo.astype(jnp.bfloat16)


def attention_weights(lengths, own, came, squares):
    whole = pl.BlockSpec(memory_space=pltpu.VMEM)
    return pl.pallas_call(
        weigh_kernel,
        in_specs=[pl.BlockSpec(memory_space=pltpu.SMEM)] + [whole] * 3,
        out_shape=(
            jax.ShapeDtypeStruct((TOK, TOK), jnp.bfloat16),
            jax.ShapeDtypeStruct((2, TOK), jnp.float32),
        ),
        compiler_params=pltpu.CompilerParams(vmem_limit_bytes=24 * 1024 * 1024),
        cost_estimate=pl.CostEstimate(flops=500_000_000, bytes_accessed=6_000_000, transcendentals=1_000_000),
        name="attention_weights",
    )(lengths, own, came, squares)


def mix_kernel(own_ref, came_ref, expo_ref, rows_ref, out_ref):
    values = (own_ref[2 * HEAD :, :] + came_ref[...].astype(jnp.float32)) * rows_ref[0:1, :]
    values = values.astype(jnp.bfloat16)
    for part in range(TOK // CHUNK):
        cols = slice(part * CHUNK, (part + 1) * CHUNK)
        mixed = jnp.dot(values, expo_ref[:, cols], preferred_element_type=jnp.float32)
        mixed = (mixed * rows_ref[1:2, cols]).astype(jnp.bfloat16)
        out_ref[:, cols] = mixed


def mix_values(own, came, expo, rows):
    return pl.pallas_call(
        mix_kernel,
        out_shape=jax.ShapeDtypeStruct((HEAD, TOK), jnp.bfloat16),
        compiler_params=pltpu.CompilerParams(vmem_limit_bytes=20 * 1024 * 1024),
        cost_estimate=pl.CostEstimate(flops=400_000_000, bytes_accessed=7_000_000, transcendentals=0),
        name="mix_values",
    )(own, came, expo, rows)


def copy_kernel(turn_ref, *refs):
    for in_ref, out_ref in zip(refs[:NX], refs[NX:]):
        out_ref[...] = in_ref[0]


def slice_columns(turn, weight):
    width = NZ * NY * HEAD

    def column_spec(k):
        return pl.BlockSpec((1, HEAD, width), lambda i, turn_ref: (0, 0, (turn_ref[0] + k) % NX))

    return pl.pallas_call(
        copy_kernel,
        grid_spec=pltpu.PrefetchScalarGridSpec(
            num_scalar_prefetch=1,
            grid=(1,),
            in_specs=[column_spec(k) for k in range(NX)],
            out_specs=[pl.BlockSpec((HEAD, width), lambda i, turn_ref: (0, 0))] * NX,
        ),
        out_shape=[jax.ShapeDtypeStruct((HEAD, width), jnp.bfloat16)] * NX,
        compiler_params=pltpu.CompilerParams(vmem_limit_bytes=48 * 1024 * 1024),
        cost_estimate=pl.CostEstimate(flops=0, bytes_accessed=5_000_000, transcendentals=0),
        name="slice_columns",
    )(turn, *[weight] * NX)


def project_kernel(w_ref, a0_ref, a1_ref, a2_ref, a3_ref, out_ref):
    heads = jnp.concatenate([ref[...] for ref in (a0_ref, a1_ref, a2_ref, a3_ref)], axis=0)
    out_ref[...] = jnp.dot(w_ref[...], heads, preferred_element_type=jnp.float32).astype(jnp.bfloat16)


def project(weight, heads):
    rows = NZ * NY * HEAD
    return pl.pallas_call(
        project_kernel,
        grid=(TOK // CHUNK,),
        in_specs=[pl.BlockSpec((rows, NX * HEAD), lambda k: (0, 0))]
        + [pl.BlockSpec((HEAD, CHUNK), lambda k: (0, k))] * NX,
        out_specs=pl.BlockSpec((rows, CHUNK), lambda k: (0, k)),
        out_shape=jax.ShapeDtypeStruct((rows, TOK), jnp.bfloat16),
        compiler_params=pltpu.CompilerParams(vmem_limit_bytes=24 * 1024 * 1024),
        cost_estimate=pl.CostEstimate(flops=2_500_000_000, bytes_accessed=7_000_000, transcendentals=0),
        name="project",
    )(weight, *heads)


def spread_kernel(parts_ref, received_ref, up_ref, middle_ref, out_ref):
    total = received_ref[...].astype(jnp.float32)
    head_sum = parts_ref[0].astype(jnp.float32)
    for x in range(1, NZ * NY):
        head_sum += parts_ref[x].astype(jnp.float32)
    middle = (total + head_sum).astype(jnp.bfloat16)
    middle_ref[...] = middle
    middle_f = middle.astype(jnp.float32)
    squares = jnp.sum(middle_f * middle_f, axis=0, keepdims=True)
    high = squares.astype(jnp.bfloat16).astype(jnp.float32)
    low = squares - high
    rows = [high[:, k * 128 : (k + 1) * 128] for k in range(8)] + [low[:, k * 128 : (k + 1) * 128] for k in range(8)]
    tile = jnp.concatenate(rows + [jnp.zeros((8, 128), jnp.float32)], axis=0)
    out_ref[:, TOK:] = jnp.concatenate([tile] * BLOCKS, axis=0).astype(jnp.bfloat16)
    out_ref[:, :TOK] = jnp.dot(up_ref[...], middle, preferred_element_type=jnp.float32).astype(jnp.bfloat16)


def spread_call(parts, received, up):
    return pl.pallas_call(
        spread_kernel,
        out_shape=(
            jax.ShapeDtypeStruct((HEAD, TOK), jnp.bfloat16),
            jax.ShapeDtypeStruct((WIDE, TOK + EXTRA), jnp.bfloat16),
        ),
        compiler_params=pltpu.CompilerParams(vmem_limit_bytes=20 * 1024 * 1024),
        cost_estimate=pl.CostEstimate(flops=310_000_000, bytes_accessed=5_000_000, transcendentals=0),
        name="spread",
    )(parts, received, up)


def hidden_kernel(up_ref, down_ref, r_ref, out_ref):
    sums = jnp.sum(r_ref[:, TOK:].astype(jnp.float32).reshape(BLOCKS, PIECE, 128), axis=0)
    sums = sums[0:8] + sums[8:16]
    total = jnp.concatenate([sums[k : k + 1] for k in range(8)], axis=1)
    scaling = lax.rsqrt(total * (1.0 / D) + epsilon)
    for part in range(TOK // CHUNK):
        cols = slice(part * CHUNK, (part + 1) * CHUNK)
        pre = jnp.dot(up_ref[...], r_ref[:, cols], preferred_element_type=jnp.float32) * scaling[:, cols]
        hidden = 0.5 * pre * (1.0 + jnp.tanh(0.7978845608028654 * (pre + 0.044715 * (pre * pre * pre))))
        out_ref[:, cols] = jnp.dot(
            down_ref[...], hidden.astype(jnp.bfloat16), preferred_element_type=jnp.float32
        ).astype(jnp.bfloat16)


def hidden_call(up, down, pieces):
    return pl.pallas_call(
        hidden_kernel,
        out_shape=jax.ShapeDtypeStruct((WIDE, TOK), jnp.bfloat16),
        compiler_params=pltpu.CompilerParams(vmem_limit_bytes=24 * 1024 * 1024),
        cost_estimate=pl.CostEstimate(flops=2_500_000_000, bytes_accessed=6_000_000, transcendentals=1_000_000),
        name="hidden",
    )(up, down, pieces)


def final_kernel(down_ref, b_ref, middle_ref, out_ref):
    out = jnp.dot(down_ref[...], b_ref[...], preferred_element_type=jnp.float32)
    out_ref[...] = (middle_ref[...].astype(jnp.float32) + out).astype(jnp.bfloat16)


def final_call(down, pieces, middle):
    return pl.pallas_call(
        final_kernel,
        out_shape=jax.ShapeDtypeStruct((HEAD, TOK), jnp.bfloat16),
        compiler_params=pltpu.CompilerParams(vmem_limit_bytes=16 * 1024 * 1024),
        cost_estimate=pl.CostEstimate(flops=310_000_000, bytes_accessed=3_000_000, transcendentals=0),
        name="final",
    )(down, pieces, middle)


TENSOR = ("x", "z", "y")


def shift_pairs(count):
    devices = NX * NZ * NY
    return [(t, (t + devices) % (count * devices)) for t in range(count * devices)]


SWAP = [(0, 1), (1, 0)]


def around(axis, value, steps):
    return lax.ppermute(value, axis, [(at, (at + steps) % NX) for at in range(NX)])


def around_x(value, steps):
    return around("x", value, steps)


def spread_over(axis, value):
    return [value] + [around(axis, value, steps) for steps in (1, 3, 2)]


def in_order(pieces):
    return [pieces[0], pieces[1], pieces[3], pieces[2]]


def shards(
    incoming,
    scene_lengths,
    attn_gain,
    query_weight,
    key_weight,
    value_weight,
    output_weight,
    ffn_gain,
    up_first,
    up_second,
    down_first,
    down_second,
):
    everything = ("pipe",) + TENSOR
    count = lax.axis_size("pipe")
    received = lax.ppermute(incoming, everything, shift_pairs(count))
    place = lax.axis_index("z").astype(jnp.int32).reshape(1)
    weights = (attn_gain, query_weight, key_weight, value_weight)
    first = half_weights(0, PART, 1 - place, *weights)
    second = half_weights(PART, NX - PART, 1 - place, *weights)
    ahead, _, _ = lax.optimization_barrier((received, first, second))
    first = lax.ppermute(first, "z", SWAP)
    second = lax.ppermute(second, "z", SWAP)
    wide = jnp.broadcast_to(ahead[None, :, :HALF], (NX, HEAD, HALF))
    wide = lax.all_to_all(wide, "x", split_axis=0, concat_axis=0, tiled=True)
    tall = jnp.stack(in_order(spread_over("y", ahead[:, HALF:])))
    wide = in_order(spread_over("y", wide))
    tall = jnp.broadcast_to(tall[None], (NX, NY, HEAD, HALF))
    tall = lax.all_to_all(tall, "x", split_axis=0, concat_axis=0, tiled=True)
    corner = lax.axis_index("y").astype(jnp.int32).reshape(1)

    turn = lax.axis_index("x").astype(jnp.int32).reshape(1)
    tied = (first, *weights, output_weight, up_first, up_second, down_first, down_second, ffn_gain)
    tied = lax.optimization_barrier(tied)
    first, *weights, output_weight, up_first, up_second, down_first, down_second, ffn_gain = tied
    own_weights = half_weights(0, NX, place, *weights)
    columns = slice_columns(turn, output_weight)
    up_first = (up_first.reshape(HEAD, WIDE).T.astype(jnp.float32) * ffn_gain).astype(jnp.bfloat16)
    up_second = up_second.reshape(WIDE, WIDE).T
    down_first = down_first.reshape(WIDE, WIDE).T
    down_second = down_second.reshape(WIDE, HEAD).T
    tied = (first, own_weights, columns, up_first, up_second, down_first, down_second)
    tied = lax.optimization_barrier(tied)
    first, own_weights, columns, up_first, up_second, down_first, down_second = tied
    mark = arrival_mark(first)

    early = early_projection(corner, first, wide, tall, mark)
    second, early = lax.optimization_barrier((second, early))
    columns, early = lax.optimization_barrier((columns, early))
    crossed, crossed_values, squares = cross_projection(corner, second, wide, tall, *early)
    came = lax.ppermute(crossed, "z", SWAP)
    came_values = lax.ppermute(crossed_values, "z", SWAP)
    _, own_weights = lax.optimization_barrier((crossed, own_weights))
    own = own_projection(corner, own_weights, wide, tall)
    blocks = [columns[0]] + [around_x(columns[k], k) for k in range(1, NX)]
    out_weight = jnp.concatenate(blocks, axis=0).T

    expo, rows = attention_weights(scene_lengths, own, came, squares)
    attended = mix_values(own, came_values, expo, rows)
    heads = [attended] + [around_x(attended, k) for k in range(1, NX)]
    partial = project(out_weight, heads)
    parts = lax.all_to_all(
        partial.reshape(NZ * NY, HEAD, TOK), ("z", "y"), split_axis=0, concat_axis=0, tiled=True
    )
    middle, spread = spread_call(parts, received, up_first)
    pieces = lax.all_to_all(
        spread.reshape(BLOCKS, PIECE, TOK + EXTRA), TENSOR, split_axis=0, concat_axis=0, tiled=True
    )
    mixed_back = hidden_call(up_second, down_first, pieces.reshape(WIDE, TOK + EXTRA))
    returned = lax.all_to_all(
        mixed_back.reshape(BLOCKS, PIECE, TOK), TENSOR, split_axis=0, concat_axis=0, tiled=True
    )
    return final_call(down_second, returned.reshape(WIDE, TOK), middle)


def solution(mesh):
    devices = mesh.devices
    finer = Mesh(devices.reshape(devices.shape[0], NX, NZ, NY), ("pipe",) + TENSOR)
    return jax.shard_map(
        shards,
        mesh=finer,
        in_specs=(
            P(TENSOR, "pipe"),
            P("pipe", None),
            P("pipe", None),
            P("pipe", TENSOR, None),
            P("pipe", TENSOR, None),
            P("pipe", TENSOR, None),
            P("pipe", TENSOR, None),
            P("pipe", TENSOR),
            P("pipe", TENSOR, None, None),
            P("pipe", TENSOR, None, None),
            P("pipe", TENSOR, None, None),
            P("pipe", TENSOR, None, None),
        ),
        out_specs=P(TENSOR, "pipe"),
        check_vma=False,
    )
```
